512 devices in a mesh: grp: 16 (over x, y), sub: 32 (over z, core).
Axes of the slice: x: 4, y: 4, z: 16, core: 2. Of those that a mesh axis runs over, the one named last changes fastest.
Arguments:
- vectors: float32 [16, 256, 640, 128], P(None, 'grp', 'sub'), may hold values from -0.03125 to 0.03125
- permeability: float32 [256, 512, 128], P('grp', 'sub'), may hold values from 0.05 to 20
- counts: int32 [16, 32], P('grp', 'sub'), may hold values from 4 to 16
- ownership: int32 [16, 32], P('grp'), may hold values from 0 to 31, each once within a row
Outputs:
- coarse_rows: float32 [16, 32, 16, 144], P('grp')
The draws below stay inside these ranges and needn't reach their ends.
Inputs may be any that keep to these rules, and one draw needn't show every extreme that they name: Each subdomain keeps its first counts vectors. `ownership`: each group's row names every subdomain index of that group once.
All inputs are finite; a program needn't handle non-finite values.
Results may differ from the reference program's by a relative error of at most 0.0003.
Values sent between devices are 32-bit elements; how exact they have to be, the bound alone decides.
A program may use at most 128 MiB of HBM per device.

```python
import math
import jax
import jax.numpy as jnp
from jax import lax

KV = 16
OV = 2
CX = 16
CZ = 16
NY = 128
NX = 256
NZ = 512
ZROWS = 640
N_GRP = 16
N_SUB = 32


def with_ends(values, key, low, largest):
    longest = values.shape.index(max(values.shape))
    spots = []
    for shift in (0, 1):
        where = [jax.random.randint(jax.random.fold_in(key, axis), (), 0, length) for axis, length in enumerate(values.shape)]
        where[longest] = (where[longest] + shift) % values.shape[longest]
        spots.append(tuple(where))
    return values.at[spots[0]].set(low).at[spots[1]].set(largest)


def block_levels(own_key, shape, pieces, least, high):
    loudness = 1.0
    for dim, parts in pieces:
        draws = jax.random.uniform(jax.random.fold_in(jax.random.fold_in(own_key, 6), dim), (parts,), jnp.float32, least / len(pieces), high / len(pieces))
        loudness = loudness * jnp.repeat(jnp.exp(draws), shape[dim] // parts).reshape((-1,) + (1,) * (len(shape) - 1 - dim))
    return loudness


def noise(key, shape, deviation, limit, shards=(), kind=jnp.bfloat16):
    array = deviation * jax.random.normal(key, shape, jnp.float32)
    if shards:
        array = array * block_levels(key, shape, shards, -0.22, 0.18)
    return jnp.clip(array, -limit, limit).astype(kind)


def setup_inputs(seed: int = 0) -> dict:
    streams_of = jax.random.split(jax.random.key(seed), 5)
    vectors = noise(streams_of[0], (KV, NX, ZROWS, NY), (CX * CZ * NY) ** -0.5, 0.03125, ((1, 16), (2, 32)), jnp.float32)
    permeability = jnp.clip(jnp.exp(math.log(20.0) - 5.9914645 * jax.random.uniform(streams_of[1], (NX, NZ, NY), jnp.float32) ** block_levels(streams_of[1], (NX, NZ, NY), ((0, 16), (1, 32)), -0.2, 0.2)), 0.05, 20.0)
    counts = with_ends(jax.random.randint(streams_of[2], (N_GRP, N_SUB), KV // 4, KV + 1), jax.random.fold_in(streams_of[2], 1), KV // 4, KV).astype(jnp.int32)
    ownership = jax.vmap(lambda own: jax.random.permutation(own, N_SUB))(jax.random.split(streams_of[3], N_GRP)).reshape((N_GRP, N_SUB)).astype(jnp.int32)
    return {"vectors": vectors, "permeability": permeability, "counts": counts, "ownership": ownership}


def harmonic(first_perm, second_perm):
    return 2.0 * first_perm * second_perm / (first_perm + second_perm)


def stencil(values, perm_window):
    centre = values[:, 1:-1, 1:-1, :]
    middle_perm = perm_window[1:-1, 1:-1, :]
    result = jnp.zeros_like(centre)
    neighbours = ((values[:, 2:, 1:-1, :], perm_window[2:, 1:-1, :]),
                  (values[:, :-2, 1:-1, :], perm_window[:-2, 1:-1, :]),
                  (values[:, 1:-1, 2:, :], perm_window[1:-1, 2:, :]),
                  (values[:, 1:-1, :-2, :], perm_window[1:-1, :-2, :]))
    for beside, beside_perm in neighbours:
        result = result + harmonic(middle_perm, beside_perm) * (centre - beside)
    zero_layer = jnp.zeros_like(centre[..., :1])
    upward = jnp.concatenate([centre[..., 1:], zero_layer], axis=3)
    downward = jnp.concatenate([zero_layer, centre[..., :-1]], axis=3)
    perm_upward = jnp.concatenate([middle_perm[..., 1:], middle_perm[..., -1:]], axis=2)
    perm_downward = jnp.concatenate([middle_perm[..., :1], middle_perm[..., :-1]], axis=2)
    result = result + harmonic(middle_perm, perm_upward) * (centre - upward)
    result = result + harmonic(middle_perm, perm_downward) * (centre - downward)
    return result


def block_of(vectors, counts, group_pos, slab_pos):
    inside = ((group_pos >= 0) & (group_pos < N_GRP) & (slab_pos >= 0) & (slab_pos < N_SUB)).astype(jnp.float32)
    group_clip = jnp.clip(group_pos, 0, N_GRP - 1).astype(jnp.int32)
    slab_clip = jnp.clip(slab_pos, 0, N_SUB - 1).astype(jnp.int32)
    extent = CZ + 2 * OV
    starts = (jnp.int32(0), (group_clip * CX).astype(jnp.int32), (slab_clip * extent).astype(jnp.int32), jnp.int32(0))
    window_block = lax.dynamic_slice(vectors, starts, (KV, CX, extent, NY))
    depths = slab_clip * CZ - OV + jnp.arange(extent, dtype=jnp.int32)
    depth_keep = ((depths >= 0) & (depths < CZ * N_SUB)).astype(jnp.float32)
    vector_keep = (jnp.arange(KV, dtype=jnp.int32) < counts[group_clip, slab_clip]).astype(jnp.float32)
    return window_block * (inside * depth_keep[None, None, :, None] * vector_keep[:, None, None, None])


def coarse_row(vectors, padded_perm, counts, group_pos, slab_pos):
    extent = CZ + 2 * OV
    own_block = block_of(vectors, counts, group_pos, slab_pos)
    widened = jnp.pad(own_block, ((0, 0), (2, 2), (2, 2), (0, 0)))
    starts = ((group_pos * CX).astype(jnp.int32), (slab_pos * CZ).astype(jnp.int32), jnp.int32(0))
    perm_window = lax.dynamic_slice(padded_perm, starts, (CX + 4, extent + 4, NY))
    applied = stencil(widened, perm_window)
    blocks = []
    for step_x in (-1, 0, 1):
        for step_z in (-1, 0, 1):
            neighbour_block = block_of(vectors, counts, group_pos + step_x, slab_pos + step_z)
            canvas = jnp.pad(neighbour_block, ((0, 0), (CX + 1, CX + 1), (CZ + 1, CZ + 1), (0, 0)))
            start_x = CX - step_x * CX
            start_z = CZ - step_z * CZ
            window = canvas[:, start_x:start_x + CX + 2, start_z:start_z + extent + 2, :]
            blocks.append(jnp.einsum("axzy,bxzy->ab", applied, window, precision=lax.Precision.HIGHEST))
    return jnp.concatenate(blocks, axis=1)


def reference(vectors, permeability, counts, ownership):
    padded_perm = jnp.pad(permeability, ((2, 2), (OV + 2, OV + 2), (0, 0)), mode="edge")

    def single_row(position):
        group_pos = position // N_SUB
        owner_pos = position % N_SUB
        slab_pos = ownership[group_pos, owner_pos]
        return coarse_row(vectors, padded_perm, counts, group_pos, slab_pos)

    all_rows = lax.map(single_row, jnp.arange(N_GRP * N_SUB, dtype=jnp.int32))
    return all_rows.reshape(N_GRP, N_SUB, KV, 9 * KV)
```

```python
import functools

import jax
import jax.numpy as jnp
from jax import lax
from jax.experimental import pallas as pl
from jax.experimental.pallas import tpu as pltpu
from jax.sharding import PartitionSpec as P

MESH = pl.DeviceIdType.MESH
KV = 16
OV = 2
CX = 16
CZ = 16
NY = 128
EXT = CZ + 2 * OV
GROUP = 4
MSG = 24


def harmonic(first_perm, second_perm):
    return 2.0 * first_perm * second_perm / (first_perm + second_perm)


def split(values):
    high = values.astype(jnp.bfloat16)
    low = (values - high.astype(jnp.float32)).astype(jnp.bfloat16)
    return high, low


def stack_split(values):
    pairs = [split(value) for value in values]
    high = jnp.concatenate([pair[0] for pair in pairs], axis=1)
    low = jnp.concatenate([pair[1] for pair in pairs], axis=1)
    return jnp.concatenate([high, low], axis=0)


def gram(first, second):
    return lax.dot_general(
        first, second, (((1,), (1,)), ((), ())), preferred_element_type=jnp.float32
    )


def fold(product):
    return (product[:KV, :KV] + product[:KV, KV:]) + (product[KV:, :KV] + product[KV:, KV:])


def assemble_kernel(n_grp, n_sub, vec, perm, counts, out, z, zup, zdn, xl, xr, xd,
                    pown, pzl, pzu, pxl, pxr, pc, pe, fx, fz, fy, dg, wp1, wp2, wl, wr, msg,
                    load_sem, send_sem, recv_sem, all_send, all_recv):
    s = lax.axis_index("sub")
    g = lax.axis_index("grp")
    up, down = lax.rem(s + 1, n_sub), lax.rem(s + n_sub - 1, n_sub)
    right, left = lax.rem(g + 1, n_grp), lax.rem(g + n_grp - 1, n_grp)

    for a in range(KV):
        pltpu.make_async_copy(
            vec.at[a], z.at[pl.ds(1, CX), pl.ds(1, EXT), a, :], load_sem.at[0]
        ).start()
    pltpu.make_async_copy(perm, pown, load_sem.at[1]).start()

    barrier = pltpu.get_barrier_semaphore()
    for tg in (left, right):
        for ts in (s, up, down):
            pl.semaphore_signal(barrier, inc=1, device_id=(tg, ts), device_id_type=MESH)

    def greet(k, carry):
        pl.semaphore_signal(
            barrier, inc=1, device_id=(g, lax.rem(s + k, n_sub)), device_id_type=MESH
        )
        return carry

    lax.fori_loop(1, n_sub, greet, 0)

    zero_block = jnp.zeros((KV, NY), jnp.float32)
    for r in range(EXT + 2):
        z[0, r] = zero_block
        z[CX + 1, r] = zero_block

    def zero_ends(x, carry):
        z[x, 0] = zero_block
        z[x, EXT + 1] = zero_block
        return carry

    lax.fori_loop(1, CX + 1, zero_ends, 0)

    pl.semaphore_wait(barrier, n_sub - 1 + 6)

    def send(slot, src, dst, tg, ts):
        copy = pltpu.make_async_remote_copy(
            src_ref=src, dst_ref=dst, send_sem=send_sem.at[slot], recv_sem=recv_sem.at[slot],
            device_id=(tg, ts), device_id_type=MESH,
        )
        copy.start()
        return copy

    half = CZ // 2
    perm_copies = [
        send(0, perm.at[:, pl.ds(half, half), :], pzl, g, up),
        send(1, perm.at[:, pl.ds(0, half), :], pzu, g, down),
        send(2, perm.at[CX - 1], pxl, right, s),
        send(3, perm.at[0], pxr, left, s),
        send(4, perm.at[CX - 1, pl.ds(half, half), :], pc.at[0], right, up),
        send(5, perm.at[CX - 1, pl.ds(0, half), :], pc.at[1], right, down),
        send(6, perm.at[0, pl.ds(half, half), :], pc.at[2], left, up),
        send(7, perm.at[0, pl.ds(0, half), :], pc.at[3], left, down),
    ]

    pltpu.make_async_copy(
        z.at[pl.ds(1, CX), pl.ds(1, EXT)], z.at[pl.ds(1, CX), pl.ds(1, EXT)], load_sem.at[0]
    ).wait()
    count = counts[0, 0]
    own_rows = (lax.broadcasted_iota(jnp.int32, (KV, NY), 0) < count).astype(jnp.float32)
    low_keep = own_rows * (s > 0).astype(jnp.float32)
    high_keep = own_rows * (s < n_sub - 1).astype(jnp.float32)

    def keep_of(r):
        return low_keep if r < OV else high_keep if r >= EXT - OV else own_rows

    def mask_ends(x, carry):
        for r in (0, 1, 2, EXT - 2, EXT - 1):
            z[x, r + 1] = z[x, r + 1] * keep_of(r)
        return carry

    lax.fori_loop(1, CX + 1, mask_ends, 0)
    for x in (1, CX):
        for r in range(3, EXT - 2):
            z[x, r + 1] = z[x, r + 1] * own_rows

    all_slots = pl.ds(1, EXT)
    vec_copies = [
        send(8, z.at[pl.ds(1, CX), pl.ds(1, 3)], zup, g, down),
        send(9, z.at[pl.ds(1, CX), pl.ds(EXT - 1, 2)], zdn, g, up),
        send(10, z.at[1, all_slots], xr, left, s),
        send(11, z.at[CX, all_slots], xl, right, s),
        send(12, z.at[CX, pl.ds(EXT - 3, 4)], xd.at[0], right, up),
        send(13, z.at[CX, pl.ds(1, 4)], xd.at[1], right, down),
        send(14, z.at[1, pl.ds(EXT - 3, 4)], xd.at[2], left, up),
        send(15, z.at[1, pl.ds(1, 4)], xd.at[3], left, down),
    ]

    pltpu.make_async_copy(perm, pown, load_sem.at[1]).wait()
    for copy in perm_copies:
        copy.wait_recv()
    at_low, at_high = s == 0, s == n_sub - 1
    at_left, at_right = g == 0, g == n_grp - 1

    def fill_perm(x, carry):
        own = pown[x]
        pe[x + 1, 3 : 3 + CZ] = own
        pe[x + 1, 0:3] = jnp.where(
            at_low, jnp.broadcast_to(own[0:1], (3, NY)), pzl[x, half - 3 : half]
        )
        pe[x + 1, 3 + CZ : 6 + CZ] = jnp.where(
            at_high, jnp.broadcast_to(own[CZ - 1 : CZ], (3, NY)), pzu[x, 0:3]
        )
        return carry

    lax.fori_loop(0, CX, fill_perm, 0)
    for edge, at_edge, own_x, face, low, high in (
        (0, at_left, 1, pxl, 0, 1), (CX + 1, at_right, CX, pxr, 2, 3)
    ):
        pe[edge, 3 : 3 + CZ] = jnp.where(at_edge, pe[own_x, 3 : 3 + CZ], face[...])
        pe[edge, 1:3] = jnp.where(
            at_edge, pe[own_x, 1:3],
            jnp.where(at_low, face[0:1], pc[low, half - 2 : half]),
        )
        pe[edge, 3 + CZ : 5 + CZ] = jnp.where(
            at_edge, pe[own_x, 3 + CZ : 5 + CZ],
            jnp.where(at_high, face[CZ - 1 : CZ], pc[high, 0:2]),
        )

    lane = lax.broadcasted_iota(jnp.int32, (EXT, NY), 1)

    fx[0] = harmonic(pe[0, 1 : 1 + EXT], pe[1, 1 : 1 + EXT])

    def coefficients(x, carry):
        own = pe[x + 1, 1 : 1 + EXT]
        right_face = harmonic(own, pe[x + 2, 1 : 1 + EXT])
        z_faces = harmonic(pe[x + 1, 0 : 1 + EXT], pe[x + 1, 1 : 2 + EXT])
        fx[x + 1] = right_face
        fz[x] = z_faces
        upward = harmonic(own, pltpu.roll(own, NY - 1, 1))
        coupling = jnp.where(lane == NY - 1, 0.0, upward)
        fy[x] = coupling
        ends = jnp.where(lane == NY - 1, own, upward) + jnp.where(
            lane == 0, own, pltpu.roll(upward, 1, 1)
        )
        dg[x] = (fx[x] + right_face) + (fz[x, 0:EXT] + fz[x, 1 : 1 + EXT]) + ends
        return carry

    lax.fori_loop(0, CX, coefficients, 0)

    not_high = 1.0 - at_high.astype(jnp.float32)

    def column(x, total):
        held = {}
        for first in range(0, EXT, GROUP):
            mine, applied = [], []
            for r in range(first, first + GROUP):
                here = z[x + 1, r + 1]
                along = fy[x, r : r + 1, :]
                result = dg[x, r : r + 1, :] * here
                result = result - fx[x, r : r + 1, :] * z[x, r + 1]
                result = result - fx[x + 1, r : r + 1, :] * z[x + 2, r + 1]
                result = result - fz[x, r : r + 1, :] * z[x + 1, r]
                result = result - fz[x, r + 1 : r + 2, :] * z[x + 1, r + 2]
                result = result - along * pltpu.roll(here, NY - 1, 1)
                result = result - pltpu.roll(along * here, 1, 1)
                mine.append(here)
                applied.append(result)
                if r in (2, 3, EXT - 4, EXT - 3):
                    held[r] = result
            total = total + gram(stack_split(mine), stack_split(applied))
        face = fz[x, EXT - 2 : EXT - 1, :]
        lower = [
            held[EXT - 4],
            held[EXT - 3] + face * z[x + 1, EXT - 1],
            -(face * not_high) * z[x + 1, EXT - 2],
        ]
        wp1[x] = stack_split(lower)
        wp2[x] = stack_split([held[2], held[3]])
        return total

    total = lax.fori_loop(0, CX, column, jnp.zeros((2 * KV, 2 * KV), jnp.float32))

    left_on = 1.0 - at_left.astype(jnp.float32)
    right_on = 1.0 - at_right.astype(jnp.float32)
    for target, on, row, coef in ((wl, left_on, 1, 0), (wr, right_on, CX, CX)):
        target[...] = stack_split(
            [-(fx[coef, r : r + 1, :] * on) * z[row, r + 1] for r in range(EXT)]
        )

    row_keep = lax.broadcasted_iota(jnp.int32, (KV, KV), 0) < count
    col_keep = lax.broadcasted_iota(jnp.int32, (KV, KV), 1) < count
    blocks = {4: jnp.where(row_keep & col_keep, fold(total), 0.0)}

    vec_copies[0].wait_recv()

    def upper_pair(x, carry):
        theirs = stack_split([zup[x, 0], zup[x, 1], zup[x, 2]])
        return carry[0] + gram(wp1[x], theirs), carry[1] + gram(theirs, wp1[x])

    zeros = jnp.zeros((2 * KV, 2 * KV), jnp.float32)
    straight, turned = lax.fori_loop(0, CX, upper_pair, (zeros, zeros))
    blocks[5] = jnp.where(row_keep, fold(straight), 0.0)
    blocks[9] = jnp.where(col_keep, fold(turned), 0.0)

    vec_copies[1].wait_recv()

    def lower_pair(x, carry):
        theirs = stack_split([zdn[x, 0], zdn[x, 1]])
        return carry[0] + gram(wp2[x], theirs), carry[1] + gram(theirs, wp2[x])

    straight, turned = lax.fori_loop(0, CX, lower_pair, (zeros, zeros))
    blocks[3] = jnp.where(row_keep, fold(straight), 0.0)
    blocks[10] = jnp.where(col_keep, fold(turned), 0.0)

    for copy in vec_copies[2:]:
        copy.wait_recv()
    for base, weight, face, low, high in ((0, wl, xl, 0, 1), (6, wr, xr, 2, 3)):
        theirs = stack_split([face[r] for r in range(EXT)])
        blocks[base + 1] = jnp.where(row_keep, fold(gram(weight[...], theirs)), 0.0)
        theirs = stack_split([xd[low, r] for r in range(4)])
        blocks[base] = jnp.where(row_keep, fold(gram(weight[:, : 4 * NY], theirs)), 0.0)
        theirs = stack_split([xd[high, r] for r in range(4)])
        blocks[base + 2] = jnp.where(
            row_keep, fold(gram(weight[:, (EXT - 4) * NY :], theirs)), 0.0
        )

    msg[0:KV, :] = jnp.concatenate([blocks[i] for i in range(8)], axis=1)
    half_v = KV // 2
    gap = jnp.zeros((half_v, KV), jnp.float32)
    parts = [blocks[8][:half_v], blocks[8][half_v:], gap, blocks[9][:half_v], blocks[9][half_v:],
             blocks[10][:half_v], blocks[10][half_v:], gap]
    msg[KV:, :] = jnp.concatenate(parts, axis=1)

    def share(k, carry):
        pltpu.make_async_remote_copy(
            src_ref=msg, dst_ref=out.at[s], send_sem=all_send, recv_sem=all_recv,
            device_id=(g, lax.rem(s + k, n_sub)), device_id_type=MESH,
        ).start()
        return carry

    lax.fori_loop(1, n_sub, share, 0)
    own_copy = pltpu.make_async_copy(msg, out.at[s], load_sem.at[2])
    own_copy.start()
    for copy in perm_copies + vec_copies:
        copy.wait_send()
    own_copy.wait()
    rest = out.at[pl.ds(0, n_sub - 1)]
    pltpu.make_async_copy(rest, rest, all_recv).wait()
    pltpu.make_async_copy(rest, rest, all_send).wait()


def place_kernel(n_sub, ownership, gathered, out):
    lane = lax.broadcasted_iota(jnp.int32, (KV // 2, NY), 1)
    from_below = (lane >= 3 * KV) & (lane < 4 * KV)
    from_above = (lane >= 5 * KV) & (lane < 6 * KV)
    half_v = KV // 2

    def place(j, carry):
        s = ownership[0, j]
        below = gathered[jnp.maximum(s - 1, 0), KV:, :]
        above = gathered[jnp.minimum(s + 1, n_sub - 1), KV:, :]
        below = jnp.where(s > 0, below, 0.0)
        above = jnp.where(s < n_sub - 1, above, 0.0)
        extra = gathered[s, KV:, :]
        for part in range(2):
            shift = NY - part * KV
            if part:
                below = pltpu.roll(below, shift, 1)
                above = pltpu.roll(above, shift, 1)
                extra = pltpu.roll(extra, shift, 1)
            rows = pl.ds(part * half_v, half_v)
            main = gathered[s, rows, :]
            main = main + jnp.where(from_below, below, 0.0) + jnp.where(from_above, above, 0.0)
            out[0, j, rows, 0:NY] = main
            out[0, j, rows, NY:] = extra[:, :KV]
        return carry

    lax.fori_loop(0, n_sub, place, 0)


def per_device(n_grp, n_sub, vectors, permeability, counts, ownership):
    f32, bf16 = jnp.float32, jnp.bfloat16
    vmem = pltpu.VMEM
    gathered = pl.pallas_call(
        functools.partial(assemble_kernel, n_grp, n_sub),
        out_shape=jax.ShapeDtypeStruct((n_sub, MSG, NY), f32),
        in_specs=[
            pl.BlockSpec(memory_space=pl.ANY),
            pl.BlockSpec(memory_space=pl.ANY),
            pl.BlockSpec(memory_space=pltpu.SMEM),
        ],
        out_specs=pl.BlockSpec(memory_space=pl.ANY),
        scratch_shapes=[
            vmem((CX + 2, EXT + 2, KV, NY), f32),
            vmem((CX, 3, KV, NY), f32),
            vmem((CX, 2, KV, NY), f32),
            vmem((EXT, KV, NY), f32),
            vmem((EXT, KV, NY), f32),
            vmem((4, 4, KV, NY), f32),
            vmem((CX, CZ, NY), f32),
            vmem((CX, CZ // 2, NY), f32),
            vmem((CX, CZ // 2, NY), f32),
            vmem((CZ, NY), f32),
            vmem((CZ, NY), f32),
            vmem((4, CZ // 2, NY), f32),
            vmem((CX + 2, EXT + 4, NY), f32),
            vmem((CX + 1, EXT, NY), f32),
            vmem((CX, EXT + 1, NY), f32),
            vmem((CX, EXT, NY), f32),
            vmem((CX, EXT, NY), f32),
            vmem((CX, 2 * KV, 3 * NY), bf16),
            vmem((CX, 2 * KV, 2 * NY), bf16),
            vmem((2 * KV, EXT * NY), bf16),
            vmem((2 * KV, EXT * NY), bf16),
            vmem((MSG, NY), f32),
            pltpu.SemaphoreType.DMA((3,)),
            pltpu.SemaphoreType.DMA((16,)),
            pltpu.SemaphoreType.DMA((16,)),
            pltpu.SemaphoreType.DMA,
            pltpu.SemaphoreType.DMA,
        ],
        compiler_params=pltpu.CompilerParams(
            collective_id=0, has_side_effects=True, vmem_limit_bytes=32 << 20
        ),
    )(vectors, permeability, counts)
    return pl.pallas_call(
        functools.partial(place_kernel, n_sub),
        out_shape=jax.ShapeDtypeStruct((1, n_sub, KV, 9 * KV), f32),
        in_specs=[
            pl.BlockSpec(memory_space=pltpu.SMEM),
            pl.BlockSpec(memory_space=pltpu.VMEM),
        ],
        out_specs=pl.BlockSpec(memory_space=pltpu.VMEM),
    )(ownership, gathered)


def solution(mesh):
    in_specs = (P(None, "grp", "sub", None), P("grp", "sub", None), P("grp", "sub"), P("grp", None))
    out_specs = P("grp", None, None, None)
    return jax.shard_map(
        functools.partial(per_device, mesh.shape["grp"], mesh.shape["sub"]),
        mesh=mesh, in_specs=in_specs, out_specs=out_specs, check_vma=False,
    )
```

```python
import functools

import jax
import jax.numpy as jnp
from jax import lax
from jax.experimental import pallas as pl
from jax.experimental.pallas import tpu as pltpu
from jax.sharding import PartitionSpec as P

MESH = pl.DeviceIdType.MESH
KV = 16
OV = 2
CX = 16
CZ = 16
NY = 128
EXT = CZ + 2 * OV
GROUP = 4
MSG = 24


def harmonic(first_perm, second_perm):
    return 2.0 * first_perm * second_perm / (first_perm + second_perm)


def split(values):
    high = values.astype(jnp.bfloat16)
    low = (values - high.astype(jnp.float32)).astype(jnp.bfloat16)
    return high, low


def stack_split(values):
    pairs = [split(value) for value in values]
    high = jnp.concatenate([pair[0] for pair in pairs], axis=1)
    low = jnp.concatenate([pair[1] for pair in pairs], axis=1)
    return jnp.concatenate([high, low], axis=0)


def gram(first, second):
    return lax.dot_general(
        first, second, (((1,), (1,)), ((), ())), preferred_element_type=jnp.float32
    )


def fold(product):
    return (product[:KV, :KV] + product[:KV, KV:]) + (product[KV:, :KV] + product[KV:, KV:])


def assemble_kernel(n_grp, n_sub, vec, perm, counts, ownership, out, z, zup, zdn, xl, xr, xd,
                    pown, pzl, pzu, pxl, pxr, pc, pe, fx, fz, fy, dg, wp1, wp2, wl, wr, pool,
                    load_sem, send_sem, recv_sem, all_send, all_recv, pair_send, pair_recv, known):
    s = lax.axis_index("sub")
    g = lax.axis_index("grp")
    up, down = lax.rem(s + 1, n_sub), lax.rem(s + n_sub - 1, n_sub)
    chip, core = s // 2, lax.rem(s, 2)
    n_chip = n_sub // 2
    mate = chip * 2 + 1 - core
    right, left = lax.rem(g + 1, n_grp), lax.rem(g + n_grp - 1, n_grp)

    for a in range(KV):
        pltpu.make_async_copy(
            vec.at[a], z.at[pl.ds(1, EXT), pl.ds(1, CX), a, :], load_sem.at[0]
        ).start()
    pltpu.make_async_copy(perm, pown, load_sem.at[1]).start()

    barrier = pltpu.get_barrier_semaphore()
    for tg in (left, right):
        for ts in (s, up, down):
            pl.semaphore_signal(barrier, inc=1, device_id=(tg, ts), device_id_type=MESH)
    for ts in (up, down):
        pl.semaphore_signal(barrier, inc=1, device_id=(g, ts), device_id_type=MESH)

    zero_block = jnp.zeros((KV, NY), jnp.float32)
    for r in range(EXT + 2):
        z[r, 0] = zero_block
        z[r, CX + 1] = zero_block

    def zero_ends(x, carry):
        z[0, x] = zero_block
        z[EXT + 1, x] = zero_block
        return carry

    lax.fori_loop(1, CX + 1, zero_ends, 0)

    pl.semaphore_wait(barrier, 8)

    def tell(step):
        reach = 1 << step
        for ts in (lax.rem(s + reach, n_sub), lax.rem(s + n_sub - reach, n_sub)):
            pl.semaphore_signal(known.at[step], inc=1, device_id=(g, ts), device_id_type=MESH)

    tell(0)

    def send(slot, src, dst, tg, ts):
        copy = pltpu.make_async_remote_copy(
            src_ref=src, dst_ref=dst, send_sem=send_sem.at[slot], recv_sem=recv_sem.at[slot],
            device_id=(tg, ts), device_id_type=MESH,
        )
        copy.start()
        return copy

    half = CZ // 2
    perm_copies = [
        send(0, perm.at[:, pl.ds(half, half), :], pzl, g, up),
        send(1, perm.at[:, pl.ds(0, half), :], pzu, g, down),
        send(2, perm.at[CX - 1], pxl, right, s),
        send(3, perm.at[0], pxr, left, s),
        send(4, perm.at[CX - 1, pl.ds(half, half), :], pc.at[0], right, up),
        send(5, perm.at[CX - 1, pl.ds(0, half), :], pc.at[1], right, down),
        send(6, perm.at[0, pl.ds(half, half), :], pc.at[2], left, up),
        send(7, perm.at[0, pl.ds(0, half), :], pc.at[3], left, down),
    ]

    pltpu.make_async_copy(
        z.at[pl.ds(1, EXT), pl.ds(1, CX)], z.at[pl.ds(1, EXT), pl.ds(1, CX)], load_sem.at[0]
    ).wait()
    count = counts[0, 0]
    own_rows = (lax.broadcasted_iota(jnp.int32, (KV, NY), 0) < count).astype(jnp.float32)
    low_keep = own_rows * (s > 0).astype(jnp.float32)
    high_keep = own_rows * (s < n_sub - 1).astype(jnp.float32)

    def keep_of(r):
        return low_keep if r < OV else high_keep if r >= EXT - OV else own_rows

    def mask_ends(x, carry):
        for r in (0, 1, 2, EXT - 2, EXT - 1):
            z[r + 1, x] = z[r + 1, x] * keep_of(r)
        return carry

    lax.fori_loop(1, CX + 1, mask_ends, 0)
    for x in (1, CX):
        for r in range(3, EXT - 2):
            z[r + 1, x] = z[r + 1, x] * own_rows

    for copy in perm_copies:
        copy.wait_send()
    all_slots = pl.ds(1, EXT)
    vec_copies = [
        send(8, z.at[pl.ds(1, 3), pl.ds(1, CX)], zup, g, down),
        send(9, z.at[pl.ds(EXT - 1, 2), pl.ds(1, CX)], zdn, g, up),
        send(10, z.at[all_slots, 1], xr, left, s),
        send(11, z.at[all_slots, CX], xl, right, s),
        send(12, z.at[pl.ds(EXT - 3, 4), CX], xd.at[0], right, up),
        send(13, z.at[pl.ds(1, 4), CX], xd.at[1], right, down),
        send(14, z.at[pl.ds(EXT - 3, 4), 1], xd.at[2], left, up),
        send(15, z.at[pl.ds(1, 4), 1], xd.at[3], left, down),
    ]

    pl.semaphore_wait(known.at[0], 2)
    tell(1)
    pltpu.make_async_copy(perm, pown, load_sem.at[1]).wait()
    for copy in perm_copies:
        copy.wait_recv()
    pl.semaphore_wait(known.at[1], 2)
    tell(2)
    at_low, at_high = s == 0, s == n_sub - 1
    at_left, at_right = g == 0, g == n_grp - 1

    def fill_perm(x, carry):
        own = pown[x]
        pe[x + 1, 3 : 3 + CZ] = own
        pe[x + 1, 0:3] = jnp.where(
            at_low, jnp.broadcast_to(own[0:1], (3, NY)), pzl[x, half - 3 : half]
        )
        pe[x + 1, 3 + CZ : 6 + CZ] = jnp.where(
            at_high, jnp.broadcast_to(own[CZ - 1 : CZ], (3, NY)), pzu[x, 0:3]
        )
        return carry

    lax.fori_loop(0, CX, fill_perm, 0)
    for edge, at_edge, own_x, face, low, high in (
        (0, at_left, 1, pxl, 0, 1), (CX + 1, at_right, CX, pxr, 2, 3)
    ):
        pe[edge, 3 : 3 + CZ] = jnp.where(at_edge, pe[own_x, 3 : 3 + CZ], face[...])
        pe[edge, 1:3] = jnp.where(
            at_edge, pe[own_x, 1:3],
            jnp.where(at_low, face[0:1], pc[low, half - 2 : half]),
        )
        pe[edge, 3 + CZ : 5 + CZ] = jnp.where(
            at_edge, pe[own_x, 3 + CZ : 5 + CZ],
            jnp.where(at_high, face[CZ - 1 : CZ], pc[high, 0:2]),
        )

    lane = lax.broadcasted_iota(jnp.int32, (EXT, NY), 1)

    fx[0] = harmonic(pe[0, 1 : 1 + EXT], pe[1, 1 : 1 + EXT])

    def coefficients(x, carry):
        own = pe[x + 1, 1 : 1 + EXT]
        right_face = harmonic(own, pe[x + 2, 1 : 1 + EXT])
        z_faces = harmonic(pe[x + 1, 0 : 1 + EXT], pe[x + 1, 1 : 2 + EXT])
        fx[x + 1] = right_face
        fz[x] = z_faces
        upward = harmonic(own, pltpu.roll(own, NY - 1, 1))
        coupling = jnp.where(lane == NY - 1, 0.0, upward)
        fy[x] = coupling
        ends = jnp.where(lane == NY - 1, own, upward) + jnp.where(
            lane == 0, own, pltpu.roll(upward, 1, 1)
        )
        dg[x] = (fx[x] + right_face) + (fz[x, 0:EXT] + fz[x, 1 : 1 + EXT]) + ends
        return carry

    lax.fori_loop(0, CX, coefficients, 0)

    not_high = 1.0 - at_high.astype(jnp.float32)

    def column(x, total):
        held = {}
        for first in range(0, EXT, GROUP):
            mine, applied = [], []
            for r in range(first, first + GROUP):
                here = z[r + 1, x + 1]
                along = fy[x, r : r + 1, :]
                result = dg[x, r : r + 1, :] * here
                result = result - fx[x, r : r + 1, :] * z[r + 1, x]
                result = result - fx[x + 1, r : r + 1, :] * z[r + 1, x + 2]
                result = result - fz[x, r : r + 1, :] * z[r, x + 1]
                result = result - fz[x, r + 1 : r + 2, :] * z[r + 2, x + 1]
                result = result - along * pltpu.roll(here, NY - 1, 1)
                result = result - pltpu.roll(along * here, 1, 1)
                mine.append(here)
                applied.append(result)
                if r in (2, 3, EXT - 4, EXT - 3):
                    held[r] = result
            total = total + gram(stack_split(mine), stack_split(applied))
        face = fz[x, EXT - 2 : EXT - 1, :]
        lower = [
            held[EXT - 4],
            held[EXT - 3] + face * z[EXT - 1, x + 1],
            -(face * not_high) * z[EXT - 2, x + 1],
        ]
        wp1[x] = stack_split(lower)
        wp2[x] = stack_split([held[2], held[3]])
        return total

    total = lax.fori_loop(0, CX // 2, column, jnp.zeros((2 * KV, 2 * KV), jnp.float32))
    pl.semaphore_wait(known.at[2], 2)
    tell(3)
    total = lax.fori_loop(CX // 2, CX, column, total)

    left_on = 1.0 - at_left.astype(jnp.float32)
    right_on = 1.0 - at_right.astype(jnp.float32)
    for target, on, row, coef in ((wl, left_on, 1, 0), (wr, right_on, CX, CX)):
        target[...] = stack_split(
            [-(fx[coef, r : r + 1, :] * on) * z[r + 1, row] for r in range(EXT)]
        )

    row_keep = lax.broadcasted_iota(jnp.int32, (KV, KV), 0) < count
    col_keep = lax.broadcasted_iota(jnp.int32, (KV, KV), 1) < count
    blocks = {4: jnp.where(row_keep & col_keep, fold(total), 0.0)}

    vec_copies[0].wait_recv()

    def upper_pair(x, carry):
        theirs = stack_split([zup[0, x], zup[1, x], zup[2, x]])
        return carry[0] + gram(wp1[x], theirs), carry[1] + gram(theirs, wp1[x])

    zeros = jnp.zeros((2 * KV, 2 * KV), jnp.float32)
    straight, turned = lax.fori_loop(0, CX, upper_pair, (zeros, zeros))
    blocks[5] = jnp.where(row_keep, fold(straight), 0.0)
    blocks[9] = jnp.where(col_keep, fold(turned), 0.0)

    vec_copies[1].wait_recv()

    def lower_pair(x, carry):
        theirs = stack_split([zdn[0, x], zdn[1, x]])
        return carry[0] + gram(wp2[x], theirs), carry[1] + gram(theirs, wp2[x])

    straight, turned = lax.fori_loop(0, CX, lower_pair, (zeros, zeros))
    blocks[3] = jnp.where(row_keep, fold(straight), 0.0)
    blocks[10] = jnp.where(col_keep, fold(turned), 0.0)

    for copy in vec_copies[2:]:
        copy.wait_recv()
    for base, weight, face, low, high in ((0, wl, xl, 0, 1), (6, wr, xr, 2, 3)):
        theirs = stack_split([face[r] for r in range(EXT)])
        blocks[base + 1] = jnp.where(row_keep, fold(gram(weight[...], theirs)), 0.0)
        theirs = stack_split([xd[low, r] for r in range(4)])
        blocks[base] = jnp.where(row_keep, fold(gram(weight[:, : 4 * NY], theirs)), 0.0)
        theirs = stack_split([xd[high, r] for r in range(4)])
        blocks[base + 2] = jnp.where(
            row_keep, fold(gram(weight[:, (EXT - 4) * NY :], theirs)), 0.0
        )

    msg = pool.at[chip, core]
    msg[0:KV, :] = jnp.concatenate([blocks[i] for i in range(8)], axis=1)
    half_v = KV // 2
    gap = jnp.zeros((half_v, KV), jnp.float32)
    parts = [blocks[8][:half_v], blocks[8][half_v:], gap, blocks[9][:half_v], blocks[9][half_v:],
             blocks[10][:half_v], blocks[10][half_v:], gap]
    msg[KV:, :] = jnp.concatenate(parts, axis=1)

    pl.semaphore_wait(known.at[3], 2)

    def share(k, carry):
        pltpu.make_async_remote_copy(
            src_ref=msg, dst_ref=msg, send_sem=all_send, recv_sem=all_recv,
            device_id=(g, lax.rem(s + n_sub // 2 + 2 * k, n_sub)), device_id_type=MESH,
        ).start()
        return carry

    lax.fori_loop(0, n_chip // 2, share, 0)
    lax.fori_loop(n_chip // 2 + 1, n_chip, share, 0)
    for copy in vec_copies:
        copy.wait_send()
    rest = pool.at[pl.ds(0, n_chip - 1), 0]
    pltpu.make_async_copy(rest, rest, all_recv).wait()
    mine = pool.at[:, core]
    pair = pltpu.make_async_remote_copy(
        src_ref=mine, dst_ref=mine, send_sem=pair_send, recv_sem=pair_recv,
        device_id=(g, mate), device_id_type=MESH,
    )
    pair.start()
    pair.wait_recv()

    lane = lax.broadcasted_iota(jnp.int32, (half_v, NY), 1)
    from_below = (lane >= 3 * KV) & (lane < 4 * KV)
    from_above = (lane >= 5 * KV) & (lane < 6 * KV)

    def place(j, carry):
        row = ownership[0, j]
        before, after = jnp.maximum(row - 1, 0), jnp.minimum(row + 1, n_sub - 1)
        below = pool[before // 2, lax.rem(before, 2), KV:, :]
        above = pool[after // 2, lax.rem(after, 2), KV:, :]
        extra = pool[row // 2, lax.rem(row, 2), KV:, :]
        added = jnp.where(from_below & (row > 0), below, 0.0)
        added = added + jnp.where(from_above & (row < n_sub - 1), above, 0.0)
        top = pool[row // 2, lax.rem(row, 2), :half_v, :]
        bottom = pool[row // 2, lax.rem(row, 2), half_v:KV, :]
        shift = NY - KV
        below = pltpu.roll(below, shift, 1)
        above = pltpu.roll(above, shift, 1)
        out[0, j, :half_v, NY:] = extra[:, :KV]
        out[0, j, half_v:, NY:] = pltpu.roll(extra, shift, 1)[:, :KV]
        out[0, j, :half_v, 0:NY] = top + added
        added = jnp.where(from_below & (row > 0), below, 0.0)
        added = added + jnp.where(from_above & (row < n_sub - 1), above, 0.0)
        out[0, j, half_v:, 0:NY] = bottom + added
        return carry

    lax.fori_loop(0, n_sub, place, 0, unroll=8)
    pair.wait_send()
    pltpu.make_async_copy(rest, rest, all_send).wait()


def per_device(n_grp, n_sub, vectors, permeability, counts, ownership):
    f32, bf16 = jnp.float32, jnp.bfloat16
    vmem = pltpu.VMEM
    return pl.pallas_call(
        functools.partial(assemble_kernel, n_grp, n_sub),
        out_shape=jax.ShapeDtypeStruct((1, n_sub, KV, 9 * KV), f32),
        in_specs=[
            pl.BlockSpec(memory_space=pl.ANY),
            pl.BlockSpec(memory_space=pl.ANY),
            pl.BlockSpec(memory_space=pltpu.SMEM),
            pl.BlockSpec(memory_space=pltpu.SMEM),
        ],
        out_specs=pl.BlockSpec(memory_space=pltpu.VMEM),
        scratch_shapes=[
            vmem((EXT + 2, CX + 2, KV, NY), f32),
            vmem((3, CX, KV, NY), f32),
            vmem((2, CX, KV, NY), f32),
            vmem((EXT, KV, NY), f32),
            vmem((EXT, KV, NY), f32),
            vmem((4, 4, KV, NY), f32),
            vmem((CX, CZ, NY), f32),
            vmem((CX, CZ // 2, NY), f32),
            vmem((CX, CZ // 2, NY), f32),
            vmem((CZ, NY), f32),
            vmem((CZ, NY), f32),
            vmem((4, CZ // 2, NY), f32),
            vmem((CX + 2, EXT + 4, NY), f32),
            vmem((CX + 1, EXT, NY), f32),
            vmem((CX, EXT + 1, NY), f32),
            vmem((CX, EXT, NY), f32),
            vmem((CX, EXT, NY), f32),
            vmem((CX, 2 * KV, 3 * NY), bf16),
            vmem((CX, 2 * KV, 2 * NY), bf16),
            vmem((2 * KV, EXT * NY), bf16),
            vmem((2 * KV, EXT * NY), bf16),
            vmem((n_sub // 2, 2, MSG, NY), f32),
            pltpu.SemaphoreType.DMA((2,)),
            pltpu.SemaphoreType.DMA((16,)),
            pltpu.SemaphoreType.DMA((16,)),
            pltpu.SemaphoreType.DMA,
            pltpu.SemaphoreType.DMA,
            pltpu.SemaphoreType.DMA,
            pltpu.SemaphoreType.DMA,
            pltpu.SemaphoreType.REGULAR((4,)),
        ],
        compiler_params=pltpu.CompilerParams(
            collective_id=0, has_side_effects=True, vmem_limit_bytes=58 << 20
        ),
    )(jnp.transpose(vectors, (0, 2, 1, 3)), permeability, counts, ownership)


def solution(mesh):
    in_specs = (P(None, "grp", "sub", None), P("grp", "sub", None), P("grp", "sub"), P("grp", None))
    out_specs = P("grp", None, None, None)
    return jax.shard_map(
        functools.partial(per_device, mesh.shape["grp"], mesh.shape["sub"]),
        mesh=mesh, in_specs=in_specs, out_specs=out_specs, check_vma=False,
    )
```

```python
import functools

import jax
import jax.numpy as jnp
from jax import lax
from jax.experimental import pallas as pl
from jax.experimental.pallas import tpu as pltpu
from jax.sharding import PartitionSpec as P

MESH = pl.DeviceIdType.MESH
KV = 16
OV = 2
CX = 16
CZ = 16
NY = 128
EXT = CZ + 2 * OV
GROUP = 4
MSG = 24


def harmonic(first_perm, second_perm):
    return 2.0 * first_perm * second_perm / (first_perm + second_perm)


def split(values):
    high = values.astype(jnp.bfloat16)
    low = (values - high.astype(jnp.float32)).astype(jnp.bfloat16)
    return high, low


def stack_split(values):
    pairs = [split(value) for value in values]
    high = jnp.concatenate([pair[0] for pair in pairs], axis=1)
    low = jnp.concatenate([pair[1] for pair in pairs], axis=1)
    return jnp.concatenate([high, low], axis=0)


def gram(first, second):
    return lax.dot_general(
        first, second, (((1,), (1,)), ((), ())), preferred_element_type=jnp.float32
    )


def fold(product):
    return (product[:KV, :KV] + product[:KV, KV:]) + (product[KV:, :KV] + product[KV:, KV:])


def assemble_kernel(n_grp, n_sub, vec, perm, counts, ownership, out, z, zup, zdn, xl, xr, xd,
                    pown, pzl, pzu, pxl, pxr, pc, fx, fz, fy, dg, ends, ex, ez, ey, ed, rim,
                    raw, wp1, wp2, wl, wr, pool,
                    load_sem, send_sem, recv_sem, all_send, all_recv, pair_send, pair_recv, known):
    s = lax.axis_index("sub")
    g = lax.axis_index("grp")
    up, down = lax.rem(s + 1, n_sub), lax.rem(s + n_sub - 1, n_sub)
    chip, core = s // 2, lax.rem(s, 2)
    n_chip = n_sub // 2
    mate = chip * 2 + 1 - core
    right, left = lax.rem(g + 1, n_grp), lax.rem(g + n_grp - 1, n_grp)

    for a in range(KV):
        pltpu.make_async_copy(
            vec.at[a], z.at[:, pl.ds(1, CX), a, :], load_sem.at[0]
        ).start()
    pltpu.make_async_copy(perm, pown, load_sem.at[1]).start()

    barrier = pltpu.get_barrier_semaphore()
    for tg in (left, right):
        for ts in (s, up, down):
            pl.semaphore_signal(barrier, inc=1, device_id=(tg, ts), device_id_type=MESH)
    for ts in (up, down):
        pl.semaphore_signal(barrier, inc=1, device_id=(g, ts), device_id_type=MESH)

    zero_block = jnp.zeros((KV, NY), jnp.float32)
    for r in range(EXT):
        z[r, 0] = zero_block
        z[r, CX + 1] = zero_block

    at_low, at_high = s == 0, s == n_sub - 1
    at_left, at_right = g == 0, g == n_grp - 1
    lane = lax.broadcasted_iota(jnp.int32, (CZ, NY), 1)
    level = lax.broadcasted_iota(jnp.int32, (CZ, NY), 0)

    def along_y(cells, lanes):
        upward = harmonic(cells, pltpu.roll(cells, NY - 1, 1))
        coupling = jnp.where(lanes == NY - 1, 0.0, upward)
        both = jnp.where(lanes == NY - 1, cells, upward) + jnp.where(
            lanes == 0, cells, pltpu.roll(upward, 1, 1)
        )
        return coupling, both

    pltpu.make_async_copy(perm, pown, load_sem.at[1]).wait()
    fx[0] = jnp.zeros((CZ, NY), jnp.float32)
    fx[CX] = jnp.zeros((CZ, NY), jnp.float32)

    def inner_faces(x, carry):
        fx[x] = harmonic(pown[x - 1], pown[x])
        return carry

    lax.fori_loop(1, CX, inner_faces, 0, unroll=5)

    def inner_coefficients(x, carry):
        own = pown[x]
        upward = jnp.where(level == CZ - 1, 0.0, harmonic(own, pltpu.roll(own, CZ - 1, 0)))
        coupling, both = along_y(own, lane)
        fz[x] = upward
        fy[x] = coupling
        dg[x] = (fx[x] + fx[x + 1]) + (upward + pltpu.roll(upward, 1, 0)) + both
        return carry

    lax.fori_loop(0, CX, inner_coefficients, 0, unroll=8)

    whole = z.at[:, pl.ds(1, CX)]
    pltpu.make_async_copy(whole, whole, load_sem.at[0]).wait()
    count = counts[0, 0]
    own_rows = (lax.broadcasted_iota(jnp.int32, (KV, NY), 0) < count).astype(jnp.float32)
    low_keep = own_rows * (s > 0).astype(jnp.float32)
    high_keep = own_rows * (s < n_sub - 1).astype(jnp.float32)

    def keep_of(r):
        return low_keep if r < OV else high_keep if r >= EXT - OV else own_rows

    def mask_ends(x, carry):
        for r in (0, 1, 2, EXT - 2, EXT - 1):
            z[r, x] = z[r, x] * keep_of(r)
        return carry

    lax.fori_loop(1, CX + 1, mask_ends, 0, unroll=4)

    def mask_sides(r, carry):
        z[r, 1] = z[r, 1] * own_rows
        z[r, CX] = z[r, CX] * own_rows
        return carry

    lax.fori_loop(3, EXT - 2, mask_sides, 0, unroll=5)

    pl.semaphore_wait(barrier, 8)

    def tell(step):
        reach = 1 << step
        for ts in (lax.rem(s + reach, n_sub), lax.rem(s + n_sub - reach, n_sub)):
            pl.semaphore_signal(known.at[step], inc=1, device_id=(g, ts), device_id_type=MESH)

    def send(slot, src, dst, tg, ts):
        copy = pltpu.make_async_remote_copy(
            src_ref=src, dst_ref=dst, send_sem=send_sem.at[slot], recv_sem=recv_sem.at[slot],
            device_id=(tg, ts), device_id_type=MESH,
        )
        copy.start()
        return copy

    half = CZ // 2
    perm_copies = [
        send(0, perm.at[:, pl.ds(half, half), :], pzl, g, up),
        send(1, perm.at[:, pl.ds(0, half), :], pzu, g, down),
        send(2, perm.at[CX - 1], pxl, right, s),
        send(3, perm.at[0], pxr, left, s),
        send(4, perm.at[CX - 1, pl.ds(half, half), :], pc.at[0], right, up),
        send(5, perm.at[CX - 1, pl.ds(0, half), :], pc.at[1], right, down),
        send(6, perm.at[0, pl.ds(half, half), :], pc.at[2], left, up),
        send(7, perm.at[0, pl.ds(0, half), :], pc.at[3], left, down),
    ]
    vec_copies = [
        send(8, z.at[pl.ds(0, 3), pl.ds(1, CX)], zup, g, down),
        send(9, z.at[pl.ds(EXT - 2, 2), pl.ds(1, CX)], zdn, g, up),
        send(10, z.at[:, 1], xr, left, s),
        send(11, z.at[:, CX], xl, right, s),
        send(12, z.at[pl.ds(EXT - 4, 4), CX], xd.at[0], right, up),
        send(13, z.at[pl.ds(0, 4), CX], xd.at[1], right, down),
        send(14, z.at[pl.ds(EXT - 4, 4), 1], xd.at[2], left, up),
        send(15, z.at[pl.ds(0, 4), 1], xd.at[3], left, down),
    ]
    tell(0)

    def column(x, total):
        for first in range(0, CZ, GROUP):
            mine, applied = [], []
            for i in range(first, first + GROUP):
                r = i + OV
                here = z[r, x + 1]
                along = fy[x, i : i + 1, :]
                result = dg[x, i : i + 1, :] * here
                result = result - fx[x, i : i + 1, :] * z[r, x]
                result = result - fx[x + 1, i : i + 1, :] * z[r, x + 2]
                if i > 0:
                    result = result - fz[x, i - 1 : i, :] * z[r - 1, x + 1]
                if i < CZ - 1:
                    result = result - fz[x, i : i + 1, :] * z[r + 1, x + 1]
                result = result - along * pltpu.roll(here, NY - 1, 1)
                result = result - pltpu.roll(along * here, 1, 1)
                mine.append(here)
                applied.append(result)
                if i < 2:
                    raw[x, i] = result
                if i >= CZ - 2:
                    raw[x, i - CZ + 4] = result
            total = total + gram(stack_split(mine), stack_split(applied))
        return total

    total = jnp.zeros((2 * KV, 2 * KV), jnp.float32)
    total = lax.fori_loop(0, 4, column, total, unroll=2)
    pl.semaphore_wait(known.at[0], 2)
    tell(1)
    total = lax.fori_loop(4, 10, column, total, unroll=2)
    pl.semaphore_wait(known.at[1], 2)
    tell(2)
    total = lax.fori_loop(10, CX, column, total, unroll=2)

    for copy in perm_copies:
        copy.wait_recv()

    def gather_ends(x, carry):
        own = pown[x]
        first, last = own[0:1], own[CZ - 1 : CZ]
        low = jnp.where(at_low, jnp.broadcast_to(first, (3, NY)), pzl[x, half - 3 : half])
        high = jnp.where(at_high, jnp.broadcast_to(last, (3, NY)), pzu[x, 0:3])
        ends[x, 0:3] = low
        ends[x, 3:4] = first
        ends[x, 4:5] = last
        ends[x, 5:8] = high
        return carry

    lax.fori_loop(0, CX, gather_ends, 0, unroll=8)
    ex[0] = jnp.zeros((8, NY), jnp.float32)
    ex[CX] = jnp.zeros((8, NY), jnp.float32)

    def end_faces(x, carry):
        ex[x] = harmonic(ends[x - 1], ends[x])
        return carry

    lax.fori_loop(1, CX, end_faces, 0, unroll=15)

    def end_coefficients(x, carry):
        own = ends[x]
        upward = harmonic(own, pltpu.roll(own, 7, 0))
        coupling, both = along_y(own, lane[0:8])
        ez[x] = upward
        ey[x] = coupling
        ed[x] = (ex[x] + ex[x + 1]) + (upward + pltpu.roll(upward, 1, 0)) + both
        return carry

    lax.fori_loop(0, CX, end_coefficients, 0, unroll=16)
    for side, at_edge, own_x, face, low, high in (
        (0, at_left, 0, pxl, 0, 1), (1, at_right, CX - 1, pxr, 2, 3)
    ):
        rim[side, 2 : 2 + CZ] = harmonic(
            pown[own_x], jnp.where(at_edge, pown[own_x], face[...])
        )
        own = ends[own_x, 1:3]
        rim[side, 0:2] = harmonic(own, jnp.where(at_edge, own, pc[low, half - 2 : half]))
        own = ends[own_x, 5:7]
        rim[side, EXT - 2 : EXT] = harmonic(own, jnp.where(at_edge, own, pc[high, 0:2]))

    not_high = 1.0 - at_high.astype(jnp.float32)

    def end_column(x, total):
        mine = {r: z[r, x + 1] for r in (0, 1, 2, EXT - 3, EXT - 2, EXT - 1)}
        applied = {}
        for r, i in ((0, 1), (1, 2), (EXT - 2, 5), (EXT - 1, 6)):
            here = mine[r]
            along = ey[x, i : i + 1, :]
            result = ed[x, i : i + 1, :] * here
            result = result - ex[x, i : i + 1, :] * z[r, x]
            result = result - ex[x + 1, i : i + 1, :] * z[r, x + 2]
            if r > 0:
                result = result - ez[x, i - 1 : i, :] * mine[r - 1]
            if r < EXT - 1:
                result = result - ez[x, i : i + 1, :] * mine[r + 1]
            result = result - along * pltpu.roll(here, NY - 1, 1)
            applied[r] = result - pltpu.roll(along * here, 1, 1)
        low_face, high_face = ez[x, 2:3, :], ez[x, 4:5, :]
        applied[2] = low_face * (mine[2] - mine[1])
        kept = high_face * mine[EXT - 3]
        applied[EXT - 3] = kept - high_face * mine[EXT - 2]
        raw[x, 0] = raw[x, 0] + applied[2]
        raw[x, 3] = raw[x, 3] + kept
        raw[x, 4] = -(kept * not_high)
        order = sorted(mine)
        return total + gram(
            stack_split([mine[r] for r in order]), stack_split([applied[r] for r in order])
        )

    total = lax.fori_loop(0, CX, end_column, total, unroll=4)
    pl.semaphore_wait(known.at[2], 2)
    tell(3)

    for target, side, row in ((wl, 0, 1), (wr, 1, CX)):
        def side_weight(i, total, target=target, side=side, row=row):
            mine, weight = [], []
            for k in range(GROUP):
                here = z[i * GROUP + k, row]
                mine.append(here)
                weight.append(rim[side, pl.ds(i * GROUP + k, 1), :] * here)
            weight = stack_split(weight)
            target[i] = weight
            return total + gram(stack_split(mine), weight)

        total = lax.fori_loop(0, EXT // GROUP, side_weight, total, unroll=5)
        for i, r in ((0, 2), (1, 3), (2, EXT - 4), (3, EXT - 3)):
            raw[row - 1, i] = raw[row - 1, i] + rim[side, r : r + 1, :] * z[r, row]

    def finish_weights(x, carry):
        wp2[x] = stack_split([raw[x, 0], raw[x, 1]])
        wp1[x] = stack_split([raw[x, 2], raw[x, 3], raw[x, 4]])
        return carry

    lax.fori_loop(0, CX, finish_weights, 0, unroll=8)

    row_keep = lax.broadcasted_iota(jnp.int32, (KV, KV), 0) < count
    col_keep = lax.broadcasted_iota(jnp.int32, (KV, KV), 1) < count
    blocks = {4: jnp.where(row_keep & col_keep, fold(total), 0.0)}

    vec_copies[0].wait_recv()

    def upper_pair(x, carry):
        theirs = stack_split([zup[0, x], zup[1, x], zup[2, x]])
        return carry[0] + gram(wp1[x], theirs), carry[1] + gram(theirs, wp1[x])

    zeros = jnp.zeros((2 * KV, 2 * KV), jnp.float32)
    straight, turned = lax.fori_loop(0, CX, upper_pair, (zeros, zeros), unroll=16)
    blocks[5] = jnp.where(row_keep, fold(straight), 0.0)
    blocks[9] = jnp.where(col_keep, fold(turned), 0.0)

    vec_copies[1].wait_recv()

    def lower_pair(x, carry):
        theirs = stack_split([zdn[0, x], zdn[1, x]])
        return carry[0] + gram(wp2[x], theirs), carry[1] + gram(theirs, wp2[x])

    straight, turned = lax.fori_loop(0, CX, lower_pair, (zeros, zeros), unroll=16)
    blocks[3] = jnp.where(row_keep, fold(straight), 0.0)
    blocks[10] = jnp.where(col_keep, fold(turned), 0.0)

    for copy in vec_copies[2:]:
        copy.wait_recv()
    left_on = -(1.0 - at_left.astype(jnp.float32))
    right_on = -(1.0 - at_right.astype(jnp.float32))
    for base, on, weight, face, low, high in ((0, left_on, wl, xl, 0, 1), (6, right_on, wr, xr, 2, 3)):
        def side_pair(i, total, weight=weight, face=face):
            theirs = stack_split([face[i * GROUP + k] for k in range(GROUP)])
            return total + gram(weight[i], theirs)

        product = lax.fori_loop(0, EXT // GROUP, side_pair, zeros, unroll=5)
        blocks[base + 1] = jnp.where(row_keep, fold(product) * on, 0.0)
        theirs = stack_split([xd[low, r] for r in range(4)])
        blocks[base] = jnp.where(row_keep, fold(gram(weight[0], theirs)) * on, 0.0)
        theirs = stack_split([xd[high, r] for r in range(4)])
        blocks[base + 2] = jnp.where(
            row_keep, fold(gram(weight[EXT // GROUP - 1], theirs)) * on, 0.0
        )

    msg = pool.at[chip, core]
    msg[0:KV, :] = jnp.concatenate([blocks[i] for i in range(8)], axis=1)
    half_v = KV // 2
    gap = jnp.zeros((half_v, KV), jnp.float32)
    parts = [blocks[8][:half_v], blocks[8][half_v:], gap, blocks[9][:half_v], blocks[9][half_v:],
             blocks[10][:half_v], blocks[10][half_v:], gap]
    msg[KV:, :] = jnp.concatenate(parts, axis=1)

    pl.semaphore_wait(known.at[3], 2)

    def share(k, carry):
        pltpu.make_async_remote_copy(
            src_ref=msg, dst_ref=msg, send_sem=all_send, recv_sem=all_recv,
            device_id=(g, lax.rem(s + n_sub // 2 + 2 * k, n_sub)), device_id_type=MESH,
        ).start()
        return carry

    lax.fori_loop(0, n_chip // 2, share, 0)
    lax.fori_loop(n_chip // 2 + 1, n_chip, share, 0)
    for copy in perm_copies + vec_copies:
        copy.wait_send()
    rest = pool.at[pl.ds(0, n_chip - 1), 0]
    pltpu.make_async_copy(rest, rest, all_recv).wait()
    mine = pool.at[:, core]
    pair = pltpu.make_async_remote_copy(
        src_ref=mine, dst_ref=mine, send_sem=pair_send, recv_sem=pair_recv,
        device_id=(g, mate), device_id_type=MESH,
    )
    pair.start()
    pair.wait_recv()

    lane = lax.broadcasted_iota(jnp.int32, (half_v, NY), 1)
    from_below = (lane >= 3 * KV) & (lane < 4 * KV)
    from_above = (lane >= 5 * KV) & (lane < 6 * KV)

    def place(j, carry):
        row = ownership[0, j]
        before, after = jnp.maximum(row - 1, 0), jnp.minimum(row + 1, n_sub - 1)
        below = pool[before // 2, lax.rem(before, 2), KV:, :]
        above = pool[after // 2, lax.rem(after, 2), KV:, :]
        extra = pool[row // 2, lax.rem(row, 2), KV:, :]
        added = jnp.where(from_below & (row > 0), below, 0.0)
        added = added + jnp.where(from_above & (row < n_sub - 1), above, 0.0)
        top = pool[row // 2, lax.rem(row, 2), :half_v, :]
        bottom = pool[row // 2, lax.rem(row, 2), half_v:KV, :]
        shift = NY - KV
        below = pltpu.roll(below, shift, 1)
        above = pltpu.roll(above, shift, 1)
        out[0, j, :half_v, NY:] = extra[:, :KV]
        out[0, j, half_v:, NY:] = pltpu.roll(extra, shift, 1)[:, :KV]
        out[0, j, :half_v, 0:NY] = top + added
        added = jnp.where(from_below & (row > 0), below, 0.0)
        added = added + jnp.where(from_above & (row < n_sub - 1), above, 0.0)
        out[0, j, half_v:, 0:NY] = bottom + added
        return carry

    lax.fori_loop(0, n_sub, place, 0, unroll=8)
    pair.wait_send()
    pltpu.make_async_copy(rest, rest, all_send).wait()


def per_device(n_grp, n_sub, vectors, permeability, counts, ownership):
    f32, bf16 = jnp.float32, jnp.bfloat16
    vmem = pltpu.VMEM
    return pl.pallas_call(
        functools.partial(assemble_kernel, n_grp, n_sub),
        out_shape=jax.ShapeDtypeStruct((1, n_sub, KV, 9 * KV), f32),
        in_specs=[
            pl.BlockSpec(memory_space=pl.ANY),
            pl.BlockSpec(memory_space=pl.ANY),
            pl.BlockSpec(memory_space=pltpu.SMEM),
            pl.BlockSpec(memory_space=pltpu.SMEM),
        ],
        out_specs=pl.BlockSpec(memory_space=pltpu.VMEM),
        scratch_shapes=[
            vmem((EXT, CX + 2, KV, NY), f32),
            vmem((3, CX, KV, NY), f32),
            vmem((2, CX, KV, NY), f32),
            vmem((EXT, KV, NY), f32),
            vmem((EXT, KV, NY), f32),
            vmem((4, 4, KV, NY), f32),
            vmem((CX, CZ, NY), f32),
            vmem((CX, CZ // 2, NY), f32),
            vmem((CX, CZ // 2, NY), f32),
            vmem((CZ, NY), f32),
            vmem((CZ, NY), f32),
            vmem((4, CZ // 2, NY), f32),
            vmem((CX + 1, CZ, NY), f32),
            vmem((CX, CZ, NY), f32),
            vmem((CX, CZ, NY), f32),
            vmem((CX, CZ, NY), f32),
            vmem((CX, 8, NY), f32),
            vmem((CX + 1, 8, NY), f32),
            vmem((CX, 8, NY), f32),
            vmem((CX, 8, NY), f32),
            vmem((CX, 8, NY), f32),
            vmem((2, EXT, NY), f32),
            vmem((CX, 5, KV, NY), f32),
            vmem((CX, 2 * KV, 3 * NY), bf16),
            vmem((CX, 2 * KV, 2 * NY), bf16),
            vmem((EXT // GROUP, 2 * KV, GROUP * NY), bf16),
            vmem((EXT // GROUP, 2 * KV, GROUP * NY), bf16),
            vmem((n_sub // 2, 2, MSG, NY), f32),
            pltpu.SemaphoreType.DMA((2,)),
            pltpu.SemaphoreType.DMA((16,)),
            pltpu.SemaphoreType.DMA((16,)),
            pltpu.SemaphoreType.DMA,
            pltpu.SemaphoreType.DMA,
            pltpu.SemaphoreType.DMA,
            pltpu.SemaphoreType.DMA,
            pltpu.SemaphoreType.REGULAR((4,)),
        ],
        compiler_params=pltpu.CompilerParams(
            collective_id=0, has_side_effects=True, vmem_limit_bytes=58 << 20
        ),
    )(jnp.transpose(vectors, (0, 2, 1, 3)), permeability, counts, ownership)


def solution(mesh):
    in_specs = (P(None, "grp", "sub", None), P("grp", "sub", None), P("grp", "sub"), P("grp", None))
    out_specs = P("grp", None, None, None)
    return jax.shard_map(
        functools.partial(per_device, mesh.shape["grp"], mesh.shape["sub"]),
        mesh=mesh, in_specs=in_specs, out_specs=out_specs, check_vma=False,
    )
```

```python
import functools

import jax
import jax.numpy as jnp
from jax import lax
from jax.experimental import pallas as pl
from jax.experimental.pallas import tpu as pltpu
from jax.sharding import PartitionSpec as P

MESH = pl.DeviceIdType.MESH
KV = 16
OV = 2
CX = 16
CZ = 16
NY = 128
EXT = CZ + 2 * OV
GROUP = 4
MSG = 24


def harmonic(first_perm, second_perm):
    return 2.0 * first_perm * second_perm / (first_perm + second_perm)


def split(values):
    high = values.astype(jnp.bfloat16)
    low = (values - high.astype(jnp.float32)).astype(jnp.bfloat16)
    return high, low


def stack_split(values):
    pairs = [split(value) for value in values]
    high = jnp.concatenate([pair[0] for pair in pairs], axis=1)
    low = jnp.concatenate([pair[1] for pair in pairs], axis=1)
    return jnp.concatenate([high, low], axis=0)


def gram(first, second):
    return lax.dot_general(
        first, second, (((1,), (1,)), ((), ())), preferred_element_type=jnp.float32
    )


def fold(product):
    return (product[:KV, :KV] + product[:KV, KV:]) + (product[KV:, :KV] + product[KV:, KV:])


def assemble_kernel(n_grp, n_sub, vec, perm, counts, ownership, out, z, zup, zdn, xl, xr, xd,
                    pown, pzl, pzu, pxl, pxr, pc, fx, fz, fy, dg, ends, ex, ez, ey, ed, rim,
                    raw, wp1, wp2, wl, wr, pool,
                    load_sem, send_sem, recv_sem, all_send, all_recv, pair_send, pair_recv, known):
    s = lax.axis_index("sub")
    g = lax.axis_index("grp")
    up, down = lax.rem(s + 1, n_sub), lax.rem(s + n_sub - 1, n_sub)
    chip, core = s // 2, lax.rem(s, 2)
    n_chip = n_sub // 2
    mate = chip * 2 + 1 - core
    right, left = lax.rem(g + 1, n_grp), lax.rem(g + n_grp - 1, n_grp)

    for a in range(KV):
        pltpu.make_async_copy(
            vec.at[a], z.at[:, pl.ds(1, CX), a, :], load_sem.at[0]
        ).start()
    pltpu.make_async_copy(perm, pown, load_sem.at[1]).start()

    barrier = pltpu.get_barrier_semaphore()
    has_left, has_right = g > 0, g < n_grp - 1
    for there, tg in ((has_left, left), (has_right, right)):
        @pl.when(there)
        def _(tg=tg):
            for ts in (s, up, down):
                pl.semaphore_signal(barrier, inc=1, device_id=(tg, ts), device_id_type=MESH)
    for reach in (1, 2, 4):
        for ts in (lax.rem(s + reach, n_sub), lax.rem(s + n_sub - reach, n_sub)):
            pl.semaphore_signal(barrier, inc=1, device_id=(g, ts), device_id_type=MESH)

    zero_block = jnp.zeros((KV, NY), jnp.float32)
    for missing, face, ring, near in (
        (g == 0, pxl, xl, (0, 1)), (g == n_grp - 1, pxr, xr, (2, 3))
    ):
        @pl.when(missing)
        def _(face=face, ring=ring, near=near):
            face[...] = jnp.zeros(face.shape, jnp.float32)
            ring[...] = jnp.zeros(ring.shape, jnp.float32)
            for i in near:
                pc[i] = jnp.zeros(pc.shape[1:], jnp.float32)
                xd[i] = jnp.zeros(xd.shape[1:], jnp.float32)

    for r in range(EXT):
        z[r, 0] = zero_block
        z[r, CX + 1] = zero_block

    at_low, at_high = s == 0, s == n_sub - 1
    at_left, at_right = g == 0, g == n_grp - 1
    lane = lax.broadcasted_iota(jnp.int32, (CZ, NY), 1)
    level = lax.broadcasted_iota(jnp.int32, (CZ, NY), 0)

    def along_y(cells, lanes):
        upward = harmonic(cells, pltpu.roll(cells, NY - 1, 1))
        coupling = jnp.where(lanes == NY - 1, 0.0, upward)
        both = jnp.where(lanes == NY - 1, cells, upward) + jnp.where(
            lanes == 0, cells, pltpu.roll(upward, 1, 1)
        )
        return coupling, both

    pltpu.make_async_copy(perm, pown, load_sem.at[1]).wait()
    fx[0] = jnp.zeros((CZ, NY), jnp.float32)
    fx[CX] = jnp.zeros((CZ, NY), jnp.float32)

    def inner_faces(x, carry):
        fx[x] = harmonic(pown[x - 1], pown[x])
        return carry

    lax.fori_loop(1, CX, inner_faces, 0, unroll=5)

    def inner_coefficients(x, carry):
        own = pown[x]
        upward = jnp.where(level == CZ - 1, 0.0, harmonic(own, pltpu.roll(own, CZ - 1, 0)))
        coupling, both = along_y(own, lane)
        fz[x] = upward
        fy[x] = coupling
        dg[x] = (fx[x] + fx[x + 1]) + (upward + pltpu.roll(upward, 1, 0)) + both
        return carry

    lax.fori_loop(0, CX, inner_coefficients, 0, unroll=8)

    whole = z.at[:, pl.ds(1, CX)]
    pltpu.make_async_copy(whole, whole, load_sem.at[0]).wait()
    count = counts[0, 0]
    own_rows = (lax.broadcasted_iota(jnp.int32, (KV, NY), 0) < count).astype(jnp.float32)
    low_keep = own_rows * (s > 0).astype(jnp.float32)
    high_keep = own_rows * (s < n_sub - 1).astype(jnp.float32)

    def keep_of(r):
        return low_keep if r < OV else high_keep if r >= EXT - OV else own_rows

    def mask_ends(x, carry):
        for r in (0, 1, 2, EXT - 2, EXT - 1):
            z[r, x] = z[r, x] * keep_of(r)
        return carry

    lax.fori_loop(1, CX + 1, mask_ends, 0, unroll=4)

    def mask_sides(r, carry):
        z[r, 1] = z[r, 1] * own_rows
        z[r, CX] = z[r, CX] * own_rows
        return carry

    lax.fori_loop(3, EXT - 2, mask_sides, 0, unroll=5)

    pl.semaphore_wait(
        barrier, 6 + 3 * has_left.astype(jnp.int32) + 3 * has_right.astype(jnp.int32)
    )

    def send(slot, src, dst, tg, ts):
        copy = pltpu.make_async_remote_copy(
            src_ref=src, dst_ref=dst, send_sem=send_sem.at[slot], recv_sem=recv_sem.at[slot],
            device_id=(tg, ts), device_id_type=MESH,
        )
        return copy

    half = CZ // 2
    perm_copies = [
        send(0, perm.at[:, pl.ds(half, half), :], pzl, g, up),
        send(1, perm.at[:, pl.ds(0, half), :], pzu, g, down),
        send(2, perm.at[CX - 1], pxl, right, s),
        send(3, perm.at[0], pxr, left, s),
        send(4, perm.at[CX - 1, pl.ds(half, half), :], pc.at[0], right, up),
        send(5, perm.at[CX - 1, pl.ds(0, half), :], pc.at[1], right, down),
        send(6, perm.at[0, pl.ds(half, half), :], pc.at[2], left, up),
        send(7, perm.at[0, pl.ds(0, half), :], pc.at[3], left, down),
    ]
    vec_copies = [
        send(8, z.at[pl.ds(0, 3), pl.ds(1, CX)], zup, g, down),
        send(9, z.at[pl.ds(EXT - 2, 2), pl.ds(1, CX)], zdn, g, up),
        send(10, z.at[:, 1], xr, left, s),
        send(11, z.at[:, CX], xl, right, s),
        send(12, z.at[pl.ds(EXT - 4, 4), CX], xd.at[0], right, up),
        send(13, z.at[pl.ds(0, 4), CX], xd.at[1], right, down),
        send(14, z.at[pl.ds(EXT - 4, 4), 1], xd.at[2], left, up),
        send(15, z.at[pl.ds(0, 4), 1], xd.at[3], left, down),
    ]
    copies = perm_copies + vec_copies
    to_left, to_right = (3, 6, 7, 10, 14, 15), (2, 4, 5, 11, 12, 13)
    along = [i for i in range(len(copies)) if i not in to_left + to_right]
    for group in (range(8), range(8, 16)):
        for slots, there in ((along, None), (to_left, has_left), (to_right, has_right)):
            def start(slots=slots, group=group):
                for i in slots:
                    if i in group:
                        copies[i].start()

            start() if there is None else pl.when(there)(start)

    def received(group):
        for slots, there in ((along, None), (to_right, has_left), (to_left, has_right)):
            def wait(slots=slots):
                for i in slots:
                    if i in group:
                        copies[i].wait_recv()

            wait() if there is None else pl.when(there)(wait)

    def sent():
        for slots, there in ((along, None), (to_left, has_left), (to_right, has_right)):
            def wait(slots=slots):
                for i in slots:
                    copies[i].wait_send()

            wait() if there is None else pl.when(there)(wait)

    for ts in (lax.rem(s + 4, n_sub), lax.rem(s + n_sub - 4, n_sub)):
        pl.semaphore_signal(known, inc=1, device_id=(g, ts), device_id_type=MESH)

    def column(x, total):
        for first in range(0, CZ, GROUP):
            mine, applied = [], []
            for i in range(first, first + GROUP):
                r = i + OV
                here = z[r, x + 1]
                along = fy[x, i : i + 1, :]
                result = dg[x, i : i + 1, :] * here
                result = result - fx[x, i : i + 1, :] * z[r, x]
                result = result - fx[x + 1, i : i + 1, :] * z[r, x + 2]
                if i > 0:
                    result = result - fz[x, i - 1 : i, :] * z[r - 1, x + 1]
                if i < CZ - 1:
                    result = result - fz[x, i : i + 1, :] * z[r + 1, x + 1]
                result = result - along * pltpu.roll(here, NY - 1, 1)
                result = result - pltpu.roll(along * here, 1, 1)
                mine.append(here)
                applied.append(result)
                if i < 2:
                    raw[x, i] = result
                if i >= CZ - 2:
                    raw[x, i - CZ + 4] = result
            total = total + gram(stack_split(mine), stack_split(applied))
        return total

    total = jnp.zeros((2 * KV, 2 * KV), jnp.float32)
    total = lax.fori_loop(0, 4, column, total, unroll=2)
    total = lax.fori_loop(4, CX, column, total, unroll=2)

    received(range(8))

    def gather_ends(x, carry):
        own = pown[x]
        first, last = own[0:1], own[CZ - 1 : CZ]
        low = jnp.where(at_low, jnp.broadcast_to(first, (3, NY)), pzl[x, half - 3 : half])
        high = jnp.where(at_high, jnp.broadcast_to(last, (3, NY)), pzu[x, 0:3])
        ends[x, 0:3] = low
        ends[x, 3:4] = first
        ends[x, 4:5] = last
        ends[x, 5:8] = high
        return carry

    lax.fori_loop(0, CX, gather_ends, 0, unroll=8)
    ex[0] = jnp.zeros((8, NY), jnp.float32)
    ex[CX] = jnp.zeros((8, NY), jnp.float32)

    def end_faces(x, carry):
        ex[x] = harmonic(ends[x - 1], ends[x])
        return carry

    lax.fori_loop(1, CX, end_faces, 0, unroll=15)

    def end_coefficients(x, carry):
        own = ends[x]
        upward = harmonic(own, pltpu.roll(own, 7, 0))
        coupling, both = along_y(own, lane[0:8])
        ez[x] = upward
        ey[x] = coupling
        ed[x] = (ex[x] + ex[x + 1]) + (upward + pltpu.roll(upward, 1, 0)) + both
        return carry

    lax.fori_loop(0, CX, end_coefficients, 0, unroll=16)
    for side, at_edge, own_x, face, low, high in (
        (0, at_left, 0, pxl, 0, 1), (1, at_right, CX - 1, pxr, 2, 3)
    ):
        rim[side, 2 : 2 + CZ] = harmonic(
            pown[own_x], jnp.where(at_edge, pown[own_x], face[...])
        )
        own = ends[own_x, 1:3]
        rim[side, 0:2] = harmonic(own, jnp.where(at_edge, own, pc[low, half - 2 : half]))
        own = ends[own_x, 5:7]
        rim[side, EXT - 2 : EXT] = harmonic(own, jnp.where(at_edge, own, pc[high, 0:2]))

    not_high = 1.0 - at_high.astype(jnp.float32)

    def end_column(x, total):
        mine = {r: z[r, x + 1] for r in (0, 1, 2, EXT - 3, EXT - 2, EXT - 1)}
        applied = {}
        for r, i in ((0, 1), (1, 2), (EXT - 2, 5), (EXT - 1, 6)):
            here = mine[r]
            along = ey[x, i : i + 1, :]
            result = ed[x, i : i + 1, :] * here
            result = result - ex[x, i : i + 1, :] * z[r, x]
            result = result - ex[x + 1, i : i + 1, :] * z[r, x + 2]
            if r > 0:
                result = result - ez[x, i - 1 : i, :] * mine[r - 1]
            if r < EXT - 1:
                result = result - ez[x, i : i + 1, :] * mine[r + 1]
            result = result - along * pltpu.roll(here, NY - 1, 1)
            applied[r] = result - pltpu.roll(along * here, 1, 1)
        low_face, high_face = ez[x, 2:3, :], ez[x, 4:5, :]
        applied[2] = low_face * (mine[2] - mine[1])
        kept = high_face * mine[EXT - 3]
        applied[EXT - 3] = kept - high_face * mine[EXT - 2]
        raw[x, 0] = raw[x, 0] + applied[2]
        raw[x, 3] = raw[x, 3] + kept
        raw[x, 4] = -(kept * not_high)
        order = sorted(mine)
        return total + gram(
            stack_split([mine[r] for r in order]), stack_split([applied[r] for r in order])
        )

    total = lax.fori_loop(0, CX, end_column, total, unroll=4)

    for target, side, row in ((wl, 0, 1), (wr, 1, CX)):
        def side_weight(i, total, target=target, side=side, row=row):
            mine, weight = [], []
            for k in range(GROUP):
                here = z[i * GROUP + k, row]
                mine.append(here)
                weight.append(rim[side, pl.ds(i * GROUP + k, 1), :] * here)
            weight = stack_split(weight)
            target[i] = weight
            return total + gram(stack_split(mine), weight)

        total = lax.fori_loop(0, EXT // GROUP, side_weight, total, unroll=5)
        for i, r in ((0, 2), (1, 3), (2, EXT - 4), (3, EXT - 3)):
            raw[row - 1, i] = raw[row - 1, i] + rim[side, r : r + 1, :] * z[r, row]

    def finish_weights(x, carry):
        wp2[x] = stack_split([raw[x, 0], raw[x, 1]])
        wp1[x] = stack_split([raw[x, 2], raw[x, 3], raw[x, 4]])
        return carry

    lax.fori_loop(0, CX, finish_weights, 0, unroll=8)

    row_keep = lax.broadcasted_iota(jnp.int32, (KV, KV), 0) < count
    col_keep = lax.broadcasted_iota(jnp.int32, (KV, KV), 1) < count
    blocks = {4: jnp.where(row_keep & col_keep, fold(total), 0.0)}

    received((8,))

    def upper_pair(x, carry):
        theirs = stack_split([zup[0, x], zup[1, x], zup[2, x]])
        return carry[0] + gram(wp1[x], theirs), carry[1] + gram(theirs, wp1[x])

    zeros = jnp.zeros((2 * KV, 2 * KV), jnp.float32)
    straight, turned = lax.fori_loop(0, CX, upper_pair, (zeros, zeros), unroll=16)
    blocks[5] = jnp.where(row_keep, fold(straight), 0.0)
    blocks[9] = jnp.where(col_keep, fold(turned), 0.0)

    received((9,))

    def lower_pair(x, carry):
        theirs = stack_split([zdn[0, x], zdn[1, x]])
        return carry[0] + gram(wp2[x], theirs), carry[1] + gram(theirs, wp2[x])

    straight, turned = lax.fori_loop(0, CX, lower_pair, (zeros, zeros), unroll=16)
    blocks[3] = jnp.where(row_keep, fold(straight), 0.0)
    blocks[10] = jnp.where(col_keep, fold(turned), 0.0)

    received(range(10, 16))
    left_on = -(1.0 - at_left.astype(jnp.float32))
    right_on = -(1.0 - at_right.astype(jnp.float32))
    for base, on, weight, face, low, high in ((0, left_on, wl, xl, 0, 1), (6, right_on, wr, xr, 2, 3)):
        def side_pair(i, total, weight=weight, face=face):
            theirs = stack_split([face[i * GROUP + k] for k in range(GROUP)])
            return total + gram(weight[i], theirs)

        product = lax.fori_loop(0, EXT // GROUP, side_pair, zeros, unroll=5)
        blocks[base + 1] = jnp.where(row_keep, fold(product) * on, 0.0)
        theirs = stack_split([xd[low, r] for r in range(4)])
        blocks[base] = jnp.where(row_keep, fold(gram(weight[0], theirs)) * on, 0.0)
        theirs = stack_split([xd[high, r] for r in range(4)])
        blocks[base + 2] = jnp.where(
            row_keep, fold(gram(weight[EXT // GROUP - 1], theirs)) * on, 0.0
        )

    msg = pool.at[chip, core]
    msg[0:KV, :] = jnp.concatenate([blocks[i] for i in range(8)], axis=1)
    half_v = KV // 2
    gap = jnp.zeros((half_v, KV), jnp.float32)
    parts = [blocks[8][:half_v], blocks[8][half_v:], gap, blocks[9][:half_v], blocks[9][half_v:],
             blocks[10][:half_v], blocks[10][half_v:], gap]
    msg[KV:, :] = jnp.concatenate(parts, axis=1)

    pl.semaphore_wait(known, 2)

    def pass_on(origin, hops):
        slot = pool.at[lax.rem(chip + n_chip + origin, n_chip), core]
        pltpu.make_async_remote_copy(
            src_ref=slot, dst_ref=slot, send_sem=all_send,
            recv_sem=all_recv.at[(origin - hops) % n_chip],
            device_id=(g, lax.rem(s + n_sub + 2 * hops, n_sub)), device_id_type=MESH,
        ).start()

    def arrived(origin):
        slot = pool.at[lax.rem(chip + n_chip + origin, n_chip), core]
        pltpu.make_async_copy(slot, slot, all_recv.at[origin % n_chip]).wait()

    def hand_over(origin):
        slot = pool.at[lax.rem(chip + n_chip + origin, n_chip), core]
        pltpu.make_async_remote_copy(
            src_ref=slot, dst_ref=slot, send_sem=pair_send, recv_sem=pair_recv,
            device_id=(g, mate), device_id_type=MESH,
        ).start()

    for hops in (4, -4, 2, -2, 1, -1):
        pass_on(0, hops)
    hand_over(0)
    arrived(-4)
    for hops in (3, 2, 1, -1):
        pass_on(-4, hops)

    @pl.when(core == 0)
    def _():
        pass_on(-4, 4)

    arrived(4)
    for hops in (-3, -2, -1, 1):
        pass_on(4, hops)

    @pl.when(core == 1)
    def _():
        pass_on(4, -4)

    hand_over(-4)
    hand_over(4)
    for origin in (1, -1, 2, -2, 3, -3, 5, -5, 6, -6, 7, -7, 8):
        arrived(origin)
        hand_over(origin)
    sent()
    theirs = pool.at[:, 0]
    pltpu.make_async_copy(theirs, theirs, pair_recv).wait()

    lane = lax.broadcasted_iota(jnp.int32, (half_v, NY), 1)
    from_below = (lane >= 3 * KV) & (lane < 4 * KV)
    from_above = (lane >= 5 * KV) & (lane < 6 * KV)

    def place(j, carry):
        row = ownership[0, j]
        before, after = jnp.maximum(row - 1, 0), jnp.minimum(row + 1, n_sub - 1)
        below = pool[before // 2, lax.rem(before, 2), KV:, :]
        above = pool[after // 2, lax.rem(after, 2), KV:, :]
        extra = pool[row // 2, lax.rem(row, 2), KV:, :]
        added = jnp.where(from_below & (row > 0), below, 0.0)
        added = added + jnp.where(from_above & (row < n_sub - 1), above, 0.0)
        top = pool[row // 2, lax.rem(row, 2), :half_v, :]
        bottom = pool[row // 2, lax.rem(row, 2), half_v:KV, :]
        shift = NY - KV
        below = pltpu.roll(below, shift, 1)
        above = pltpu.roll(above, shift, 1)
        out[0, j, :half_v, NY:] = extra[:, :KV]
        out[0, j, half_v:, NY:] = pltpu.roll(extra, shift, 1)[:, :KV]
        out[0, j, :half_v, 0:NY] = top + added
        added = jnp.where(from_below & (row > 0), below, 0.0)
        added = added + jnp.where(from_above & (row < n_sub - 1), above, 0.0)
        out[0, j, half_v:, 0:NY] = bottom + added
        return carry

    lax.fori_loop(0, n_sub, place, 0, unroll=8)
    rest = pool.at[pl.ds(0, n_chip - 1), 0]
    pltpu.make_async_copy(theirs, theirs, pair_send).wait()
    pltpu.make_async_copy(rest, rest, all_send).wait()


def per_device(n_grp, n_sub, vectors, permeability, counts, ownership):
    f32, bf16 = jnp.float32, jnp.bfloat16
    vmem = pltpu.VMEM
    return pl.pallas_call(
        functools.partial(assemble_kernel, n_grp, n_sub),
        out_shape=jax.ShapeDtypeStruct((1, n_sub, KV, 9 * KV), f32),
        in_specs=[
            pl.BlockSpec(memory_space=pl.ANY),
            pl.BlockSpec(memory_space=pl.ANY),
            pl.BlockSpec(memory_space=pltpu.SMEM),
            pl.BlockSpec(memory_space=pltpu.SMEM),
        ],
        out_specs=pl.BlockSpec(memory_space=pltpu.VMEM),
        scratch_shapes=[
            vmem((EXT, CX + 2, KV, NY), f32),
            vmem((3, CX, KV, NY), f32),
            vmem((2, CX, KV, NY), f32),
            vmem((EXT, KV, NY), f32),
            vmem((EXT, KV, NY), f32),
            vmem((4, 4, KV, NY), f32),
            vmem((CX, CZ, NY), f32),
            vmem((CX, CZ // 2, NY), f32),
            vmem((CX, CZ // 2, NY), f32),
            vmem((CZ, NY), f32),
            vmem((CZ, NY), f32),
            vmem((4, CZ // 2, NY), f32),
            vmem((CX + 1, CZ, NY), f32),
            vmem((CX, CZ, NY), f32),
            vmem((CX, CZ, NY), f32),
            vmem((CX, CZ, NY), f32),
            vmem((CX, 8, NY), f32),
            vmem((CX + 1, 8, NY), f32),
            vmem((CX, 8, NY), f32),
            vmem((CX, 8, NY), f32),
            vmem((CX, 8, NY), f32),
            vmem((2, EXT, NY), f32),
            vmem((CX, 5, KV, NY), f32),
            vmem((CX, 2 * KV, 3 * NY), bf16),
            vmem((CX, 2 * KV, 2 * NY), bf16),
            vmem((EXT // GROUP, 2 * KV, GROUP * NY), bf16),
            vmem((EXT // GROUP, 2 * KV, GROUP * NY), bf16),
            vmem((n_sub // 2, 2, MSG, NY), f32),
            pltpu.SemaphoreType.DMA((2,)),
            pltpu.SemaphoreType.DMA((16,)),
            pltpu.SemaphoreType.DMA((16,)),
            pltpu.SemaphoreType.DMA,
            pltpu.SemaphoreType.DMA((n_sub // 2,)),
            pltpu.SemaphoreType.DMA,
            pltpu.SemaphoreType.DMA,
            pltpu.SemaphoreType.REGULAR,
        ],
        compiler_params=pltpu.CompilerParams(
            collective_id=0, has_side_effects=True, vmem_limit_bytes=58 << 20
        ),
    )(jnp.transpose(vectors, (0, 2, 1, 3)), permeability, counts, ownership)


def solution(mesh):
    in_specs = (P(None, "grp", "sub", None), P("grp", "sub", None), P("grp", "sub"), P("grp", None))
    out_specs = P("grp", None, None, None)
    return jax.shard_map(
        functools.partial(per_device, mesh.shape["grp"], mesh.shape["sub"]),
        mesh=mesh, in_specs=in_specs, out_specs=out_specs, check_vma=False,
    )
```

```python
import functools

import jax
import jax.numpy as jnp
from jax import lax
from jax.experimental import pallas as pl
from jax.experimental.pallas import tpu as pltpu
from jax.sharding import PartitionSpec as P

MESH = pl.DeviceIdType.MESH
KV = 16
OV = 2
CX = 16
CZ = 16
NY = 128
EXT = CZ + 2 * OV
GROUP = 4
MSG = 24


def harmonic(first_perm, second_perm):
    return 2.0 * first_perm * second_perm / (first_perm + second_perm)


def split(values):
    high = values.astype(jnp.bfloat16)
    low = (values - high.astype(jnp.float32)).astype(jnp.bfloat16)
    return high, low


def stack_split(values):
    pairs = [split(value) for value in values]
    high = jnp.concatenate([pair[0] for pair in pairs], axis=1)
    low = jnp.concatenate([pair[1] for pair in pairs], axis=1)
    return jnp.concatenate([high, low], axis=0)


def gram(first, second):
    return lax.dot_general(
        first, second, (((1,), (1,)), ((), ())), preferred_element_type=jnp.float32
    )


def fold(product):
    return (product[:KV, :KV] + product[:KV, KV:]) + (product[KV:, :KV] + product[KV:, KV:])


def assemble_kernel(n_grp, n_sub, vec, perm, counts, ownership, out, z, zup, zdn, xl, xr, xd,
                    pown, pzl, pzu, pxl, pxr, pc, fx, fz, fy, dg, ends, ex, ez, ey, ed, rim,
                    raw, wp1, wp2, wl, wr, pool,
                    load_sem, send_sem, recv_sem, all_send, all_recv, pair_send, pair_recv, known):
    s = lax.axis_index("sub")
    g = lax.axis_index("grp")
    up, down = lax.rem(s + 1, n_sub), lax.rem(s + n_sub - 1, n_sub)
    chip, core = s // 2, lax.rem(s, 2)
    n_chip = n_sub // 2
    mate = chip * 2 + 1 - core
    right, left = lax.rem(g + 1, n_grp), lax.rem(g + n_grp - 1, n_grp)

    for a in range(KV):
        pltpu.make_async_copy(
            vec.at[a], z.at[:, pl.ds(1, CX), a, :], load_sem.at[0]
        ).start()
    pltpu.make_async_copy(perm, pown, load_sem.at[1]).start()

    barrier = pltpu.get_barrier_semaphore()
    has_left, has_right = g > 0, g < n_grp - 1
    for there, tg in ((has_left, left), (has_right, right)):
        @pl.when(there)
        def _(tg=tg):
            for ts in (s, up, down):
                pl.semaphore_signal(barrier, inc=1, device_id=(tg, ts), device_id_type=MESH)
    for reach in (1, 2, 4):
        for ts in (lax.rem(s + reach, n_sub), lax.rem(s + n_sub - reach, n_sub)):
            pl.semaphore_signal(barrier, inc=1, device_id=(g, ts), device_id_type=MESH)

    zero_block = jnp.zeros((KV, NY), jnp.float32)
    for missing, face, ring, near in (
        (g == 0, pxl, xl, (0, 1)), (g == n_grp - 1, pxr, xr, (2, 3))
    ):
        @pl.when(missing)
        def _(face=face, ring=ring, near=near):
            face[...] = jnp.zeros(face.shape, jnp.float32)
            ring[...] = jnp.zeros(ring.shape, jnp.float32)
            for i in near:
                pc[i] = jnp.zeros(pc.shape[1:], jnp.float32)
                xd[i] = jnp.zeros(xd.shape[1:], jnp.float32)

    for r in range(EXT):
        z[r, 0] = zero_block
        z[r, CX + 1] = zero_block

    at_low, at_high = s == 0, s == n_sub - 1
    at_left, at_right = g == 0, g == n_grp - 1
    lane = lax.broadcasted_iota(jnp.int32, (CZ, NY), 1)
    level = lax.broadcasted_iota(jnp.int32, (CZ, NY), 0)

    def along_y(cells, lanes):
        upward = harmonic(cells, pltpu.roll(cells, NY - 1, 1))
        coupling = jnp.where(lanes == NY - 1, 0.0, upward)
        both = jnp.where(lanes == NY - 1, cells, upward) + jnp.where(
            lanes == 0, cells, pltpu.roll(upward, 1, 1)
        )
        return coupling, both

    pltpu.make_async_copy(perm, pown, load_sem.at[1]).wait()
    fx[0] = jnp.zeros((CZ, NY), jnp.float32)
    fx[CX] = jnp.zeros((CZ, NY), jnp.float32)

    def inner_faces(x, carry):
        fx[x] = harmonic(pown[x - 1], pown[x])
        return carry

    lax.fori_loop(1, CX, inner_faces, 0, unroll=5)

    def inner_coefficients(x, carry):
        own = pown[x]
        upward = jnp.where(level == CZ - 1, 0.0, harmonic(own, pltpu.roll(own, CZ - 1, 0)))
        coupling, both = along_y(own, lane)
        fz[x] = upward
        fy[x] = coupling
        dg[x] = (fx[x] + fx[x + 1]) + (upward + pltpu.roll(upward, 1, 0)) + both
        return carry

    lax.fori_loop(0, CX, inner_coefficients, 0, unroll=8)

    pl.semaphore_wait(
        barrier, 6 + 3 * has_left.astype(jnp.int32) + 3 * has_right.astype(jnp.int32)
    )

    def send(slot, src, dst, tg, ts):
        copy = pltpu.make_async_remote_copy(
            src_ref=src, dst_ref=dst, send_sem=send_sem.at[slot], recv_sem=recv_sem.at[slot],
            device_id=(tg, ts), device_id_type=MESH,
        )
        return copy

    half = CZ // 2
    perm_copies = [
        send(0, perm.at[:, pl.ds(CZ - 3, 3), :], pzl, g, up),
        send(1, perm.at[:, pl.ds(0, 3), :], pzu, g, down),
        send(2, perm.at[CX - 1], pxl, right, s),
        send(3, perm.at[0], pxr, left, s),
        send(4, perm.at[CX - 1, pl.ds(half, half), :], pc.at[0], right, up),
        send(5, perm.at[CX - 1, pl.ds(0, half), :], pc.at[1], right, down),
        send(6, perm.at[0, pl.ds(half, half), :], pc.at[2], left, up),
        send(7, perm.at[0, pl.ds(0, half), :], pc.at[3], left, down),
    ]
    vec_copies = [
        send(8, z.at[pl.ds(0, 3), pl.ds(1, CX)], zup, g, down),
        send(9, z.at[pl.ds(EXT - 2, 2), pl.ds(1, CX)], zdn, g, up),
        send(10, z.at[:, 1], xr, left, s),
        send(11, z.at[:, CX], xl, right, s),
        send(12, z.at[pl.ds(EXT - 4, 4), CX], xd.at[0], right, up),
        send(13, z.at[pl.ds(0, 4), CX], xd.at[1], right, down),
        send(14, z.at[pl.ds(EXT - 4, 4), 1], xd.at[2], left, up),
        send(15, z.at[pl.ds(0, 4), 1], xd.at[3], left, down),
    ]
    copies = perm_copies + vec_copies
    to_left, to_right = (3, 6, 7, 10, 14, 15), (2, 4, 5, 11, 12, 13)
    along = [i for i in range(len(copies)) if i not in to_left + to_right]
    def start_all(group):
        for slots, there in ((along, None), (to_left, has_left), (to_right, has_right)):
            def start(slots=slots):
                for i in slots:
                    if i in group:
                        copies[i].start()

            start() if there is None else pl.when(there)(start)

    def received(group):
        for slots, there in ((along, None), (to_right, has_left), (to_left, has_right)):
            def wait(slots=slots):
                for i in slots:
                    if i in group:
                        copies[i].wait_recv()

            wait() if there is None else pl.when(there)(wait)

    def sent():
        for slots, there in ((along, None), (to_left, has_left), (to_right, has_right)):
            def wait(slots=slots):
                for i in slots:
                    copies[i].wait_send()

            wait() if there is None else pl.when(there)(wait)

    start_all(range(8))
    whole = z.at[:, pl.ds(1, CX)]
    pltpu.make_async_copy(whole, whole, load_sem.at[0]).wait()
    count = counts[0, 0]
    own_rows = (lax.broadcasted_iota(jnp.int32, (KV, NY), 0) < count).astype(jnp.float32)
    low_keep = own_rows * (s > 0).astype(jnp.float32)
    high_keep = own_rows * (s < n_sub - 1).astype(jnp.float32)

    def keep_of(r):
        return low_keep if r < OV else high_keep if r >= EXT - OV else own_rows

    def mask_ends(x, carry):
        for r in (0, 1, 2, EXT - 2, EXT - 1):
            z[r, x] = z[r, x] * keep_of(r)
        return carry

    lax.fori_loop(1, CX + 1, mask_ends, 0, unroll=4)

    def mask_sides(r, carry):
        z[r, 1] = z[r, 1] * own_rows
        z[r, CX] = z[r, CX] * own_rows
        return carry

    lax.fori_loop(3, EXT - 2, mask_sides, 0, unroll=5)

    start_all(range(8, 16))
    for ts in (lax.rem(s + 4, n_sub), lax.rem(s + n_sub - 4, n_sub)):
        pl.semaphore_signal(known, inc=1, device_id=(g, ts), device_id_type=MESH)

    def column(x, total):
        for first in range(0, CZ, GROUP):
            mine, applied = [], []
            for i in range(first, first + GROUP):
                r = i + OV
                here = z[r, x + 1]
                along = fy[x, i : i + 1, :]
                result = dg[x, i : i + 1, :] * here
                result = result - fx[x, i : i + 1, :] * z[r, x]
                result = result - fx[x + 1, i : i + 1, :] * z[r, x + 2]
                if i > 0:
                    result = result - fz[x, i - 1 : i, :] * z[r - 1, x + 1]
                if i < CZ - 1:
                    result = result - fz[x, i : i + 1, :] * z[r + 1, x + 1]
                result = result - along * pltpu.roll(here, NY - 1, 1)
                result = result - pltpu.roll(along * here, 1, 1)
                mine.append(here)
                applied.append(result)
                if i < 2:
                    raw[x, i] = result
                if i >= CZ - 2:
                    raw[x, i - CZ + 4] = result
            total = total + gram(stack_split(mine), stack_split(applied))
        return total

    total = jnp.zeros((2 * KV, 2 * KV), jnp.float32)
    total = lax.fori_loop(0, 4, column, total, unroll=2)
    total = lax.fori_loop(4, CX, column, total, unroll=2)

    received(range(8))

    def gather_ends(x, carry):
        own = pown[x]
        first, last = own[0:1], own[CZ - 1 : CZ]
        low = jnp.where(at_low, jnp.broadcast_to(first, (3, NY)), pzl[x])
        high = jnp.where(at_high, jnp.broadcast_to(last, (3, NY)), pzu[x])
        ends[x, 0:3] = low
        ends[x, 3:4] = first
        ends[x, 4:5] = last
        ends[x, 5:8] = high
        return carry

    lax.fori_loop(0, CX, gather_ends, 0, unroll=8)
    ex[0] = jnp.zeros((8, NY), jnp.float32)
    ex[CX] = jnp.zeros((8, NY), jnp.float32)

    def end_faces(x, carry):
        ex[x] = harmonic(ends[x - 1], ends[x])
        return carry

    lax.fori_loop(1, CX, end_faces, 0, unroll=15)

    def end_coefficients(x, carry):
        own = ends[x]
        upward = harmonic(own, pltpu.roll(own, 7, 0))
        coupling, both = along_y(own, lane[0:8])
        ez[x] = upward
        ey[x] = coupling
        ed[x] = (ex[x] + ex[x + 1]) + (upward + pltpu.roll(upward, 1, 0)) + both
        return carry

    lax.fori_loop(0, CX, end_coefficients, 0, unroll=16)
    for side, at_edge, own_x, face, low, high in (
        (0, at_left, 0, pxl, 0, 1), (1, at_right, CX - 1, pxr, 2, 3)
    ):
        rim[side, 2 : 2 + CZ] = harmonic(
            pown[own_x], jnp.where(at_edge, pown[own_x], face[...])
        )
        own = ends[own_x, 1:3]
        rim[side, 0:2] = harmonic(own, jnp.where(at_edge, own, pc[low, half - 2 : half]))
        own = ends[own_x, 5:7]
        rim[side, EXT - 2 : EXT] = harmonic(own, jnp.where(at_edge, own, pc[high, 0:2]))

    not_high = 1.0 - at_high.astype(jnp.float32)

    def end_column(x, total):
        mine = {r: z[r, x + 1] for r in (0, 1, 2, EXT - 3, EXT - 2, EXT - 1)}
        applied = {}
        for r, i in ((0, 1), (1, 2), (EXT - 2, 5), (EXT - 1, 6)):
            here = mine[r]
            along = ey[x, i : i + 1, :]
            result = ed[x, i : i + 1, :] * here
            result = result - ex[x, i : i + 1, :] * z[r, x]
            result = result - ex[x + 1, i : i + 1, :] * z[r, x + 2]
            if r > 0:
                result = result - ez[x, i - 1 : i, :] * mine[r - 1]
            if r < EXT - 1:
                result = result - ez[x, i : i + 1, :] * mine[r + 1]
            result = result - along * pltpu.roll(here, NY - 1, 1)
            applied[r] = result - pltpu.roll(along * here, 1, 1)
        low_face, high_face = ez[x, 2:3, :], ez[x, 4:5, :]
        applied[2] = low_face * (mine[2] - mine[1])
        kept = high_face * mine[EXT - 3]
        applied[EXT - 3] = kept - high_face * mine[EXT - 2]
        raw[x, 0] = raw[x, 0] + applied[2]
        raw[x, 3] = raw[x, 3] + kept
        raw[x, 4] = -(kept * not_high)
        order = sorted(mine)
        return total + gram(
            stack_split([mine[r] for r in order]), stack_split([applied[r] for r in order])
        )

    total = lax.fori_loop(0, CX, end_column, total, unroll=4)

    for target, side, row in ((wl, 0, 1), (wr, 1, CX)):
        def side_weight(i, total, target=target, side=side, row=row):
            mine, weight = [], []
            for k in range(GROUP):
                here = z[i * GROUP + k, row]
                mine.append(here)
                weight.append(rim[side, pl.ds(i * GROUP + k, 1), :] * here)
            weight = stack_split(weight)
            target[i] = weight
            return total + gram(stack_split(mine), weight)

        total = lax.fori_loop(0, EXT // GROUP, side_weight, total, unroll=5)
        for i, r in ((0, 2), (1, 3), (2, EXT - 4), (3, EXT - 3)):
            raw[row - 1, i] = raw[row - 1, i] + rim[side, r : r + 1, :] * z[r, row]

    def finish_weights(x, carry):
        wp2[x] = stack_split([raw[x, 0], raw[x, 1]])
        wp1[x] = stack_split([raw[x, 2], raw[x, 3], raw[x, 4]])
        return carry

    lax.fori_loop(0, CX, finish_weights, 0, unroll=8)

    row_keep = lax.broadcasted_iota(jnp.int32, (KV, KV), 0) < count
    col_keep = lax.broadcasted_iota(jnp.int32, (KV, KV), 1) < count
    blocks = {4: jnp.where(row_keep & col_keep, fold(total), 0.0)}

    received((8,))

    def upper_pair(x, carry):
        theirs = stack_split([zup[0, x], zup[1, x], zup[2, x]])
        return carry[0] + gram(wp1[x], theirs), carry[1] + gram(theirs, wp1[x])

    zeros = jnp.zeros((2 * KV, 2 * KV), jnp.float32)
    straight, turned = lax.fori_loop(0, CX, upper_pair, (zeros, zeros), unroll=16)
    blocks[5] = jnp.where(row_keep, fold(straight), 0.0)
    blocks[9] = jnp.where(col_keep, fold(turned), 0.0)

    received((9,))

    def lower_pair(x, carry):
        theirs = stack_split([zdn[0, x], zdn[1, x]])
        return carry[0] + gram(wp2[x], theirs), carry[1] + gram(theirs, wp2[x])

    straight, turned = lax.fori_loop(0, CX, lower_pair, (zeros, zeros), unroll=16)
    blocks[3] = jnp.where(row_keep, fold(straight), 0.0)
    blocks[10] = jnp.where(col_keep, fold(turned), 0.0)

    received(range(10, 16))
    left_on = -(1.0 - at_left.astype(jnp.float32))
    right_on = -(1.0 - at_right.astype(jnp.float32))
    for base, on, weight, face, low, high in ((0, left_on, wl, xl, 0, 1), (6, right_on, wr, xr, 2, 3)):
        def side_pair(i, total, weight=weight, face=face):
            theirs = stack_split([face[i * GROUP + k] for k in range(GROUP)])
            return total + gram(weight[i], theirs)

        product = lax.fori_loop(0, EXT // GROUP, side_pair, zeros, unroll=5)
        blocks[base + 1] = jnp.where(row_keep, fold(product) * on, 0.0)
        theirs = stack_split([xd[low, r] for r in range(4)])
        blocks[base] = jnp.where(row_keep, fold(gram(weight[0], theirs)) * on, 0.0)
        theirs = stack_split([xd[high, r] for r in range(4)])
        blocks[base + 2] = jnp.where(
            row_keep, fold(gram(weight[EXT // GROUP - 1], theirs)) * on, 0.0
        )

    msg = pool.at[chip, core]
    msg[0:KV, :] = jnp.concatenate([blocks[i] for i in range(8)], axis=1)
    half_v = KV // 2
    gap = jnp.zeros((half_v, KV), jnp.float32)
    parts = [blocks[8][:half_v], blocks[8][half_v:], gap, blocks[9][:half_v], blocks[9][half_v:],
             blocks[10][:half_v], blocks[10][half_v:], gap]
    msg[KV:, :] = jnp.concatenate(parts, axis=1)

    pl.semaphore_wait(known, 2)

    def pass_on(origin, hops):
        slot = pool.at[lax.rem(chip + n_chip + origin, n_chip), core]
        pltpu.make_async_remote_copy(
            src_ref=slot, dst_ref=slot, send_sem=all_send,
            recv_sem=all_recv.at[(origin - hops) % n_chip],
            device_id=(g, lax.rem(s + n_sub + 2 * hops, n_sub)), device_id_type=MESH,
        ).start()

    def arrived(origin):
        slot = pool.at[lax.rem(chip + n_chip + origin, n_chip), core]
        pltpu.make_async_copy(slot, slot, all_recv.at[origin % n_chip]).wait()

    def hand_over(origin):
        slot = pool.at[lax.rem(chip + n_chip + origin, n_chip), core]
        pltpu.make_async_remote_copy(
            src_ref=slot, dst_ref=slot, send_sem=pair_send, recv_sem=pair_recv,
            device_id=(g, mate), device_id_type=MESH,
        ).start()

    for hops in (4, -4, 2, -2, 1, -1):
        pass_on(0, hops)
    hand_over(0)
    arrived(-4)
    for hops in (3, 2, 1, -1):
        pass_on(-4, hops)

    @pl.when(core == 0)
    def _():
        pass_on(-4, 4)

    arrived(4)
    for hops in (-3, -2, -1, 1):
        pass_on(4, hops)

    @pl.when(core == 1)
    def _():
        pass_on(4, -4)

    hand_over(-4)
    hand_over(4)
    for origin in (1, -1, 2, -2, 3, -3, 5, -5, 6, -6, 7, -7, 8):
        arrived(origin)
        hand_over(origin)
    sent()
    theirs = pool.at[:, 0]
    pltpu.make_async_copy(theirs, theirs, pair_recv).wait()

    lane = lax.broadcasted_iota(jnp.int32, (half_v, NY), 1)
    from_below = (lane >= 3 * KV) & (lane < 4 * KV)
    from_above = (lane >= 5 * KV) & (lane < 6 * KV)

    def place(j, carry):
        row = ownership[0, j]
        before, after = jnp.maximum(row - 1, 0), jnp.minimum(row + 1, n_sub - 1)
        below = pool[before // 2, lax.rem(before, 2), KV:, :]
        above = pool[after // 2, lax.rem(after, 2), KV:, :]
        extra = pool[row // 2, lax.rem(row, 2), KV:, :]
        added = jnp.where(from_below & (row > 0), below, 0.0)
        added = added + jnp.where(from_above & (row < n_sub - 1), above, 0.0)
        top = pool[row // 2, lax.rem(row, 2), :half_v, :]
        bottom = pool[row // 2, lax.rem(row, 2), half_v:KV, :]
        shift = NY - KV
        below = pltpu.roll(below, shift, 1)
        above = pltpu.roll(above, shift, 1)
        out[0, j, :half_v, NY:] = extra[:, :KV]
        out[0, j, half_v:, NY:] = pltpu.roll(extra, shift, 1)[:, :KV]
        out[0, j, :half_v, 0:NY] = top + added
        added = jnp.where(from_below & (row > 0), below, 0.0)
        added = added + jnp.where(from_above & (row < n_sub - 1), above, 0.0)
        out[0, j, half_v:, 0:NY] = bottom + added
        return carry

    lax.fori_loop(0, n_sub, place, 0, unroll=8)
    rest = pool.at[pl.ds(0, n_chip - 1), 0]
    pltpu.make_async_copy(theirs, theirs, pair_send).wait()
    pltpu.make_async_copy(rest, rest, all_send).wait()


def per_device(n_grp, n_sub, vectors, permeability, counts, ownership):
    f32, bf16 = jnp.float32, jnp.bfloat16
    vmem = pltpu.VMEM
    return pl.pallas_call(
        functools.partial(assemble_kernel, n_grp, n_sub),
        out_shape=jax.ShapeDtypeStruct((1, n_sub, KV, 9 * KV), f32),
        in_specs=[
            pl.BlockSpec(memory_space=pl.ANY),
            pl.BlockSpec(memory_space=pl.ANY),
            pl.BlockSpec(memory_space=pltpu.SMEM),
            pl.BlockSpec(memory_space=pltpu.SMEM),
        ],
        out_specs=pl.BlockSpec(memory_space=pltpu.VMEM),
        scratch_shapes=[
            vmem((EXT, CX + 2, KV, NY), f32),
            vmem((3, CX, KV, NY), f32),
            vmem((2, CX, KV, NY), f32),
            vmem((EXT, KV, NY), f32),
            vmem((EXT, KV, NY), f32),
            vmem((4, 4, KV, NY), f32),
            vmem((CX, CZ, NY), f32),
            vmem((CX, 3, NY), f32),
            vmem((CX, 3, NY), f32),
            vmem((CZ, NY), f32),
            vmem((CZ, NY), f32),
            vmem((4, CZ // 2, NY), f32),
            vmem((CX + 1, CZ, NY), f32),
            vmem((CX, CZ, NY), f32),
            vmem((CX, CZ, NY), f32),
            vmem((CX, CZ, NY), f32),
            vmem((CX, 8, NY), f32),
            vmem((CX + 1, 8, NY), f32),
            vmem((CX, 8, NY), f32),
            vmem((CX, 8, NY), f32),
            vmem((CX, 8, NY), f32),
            vmem((2, EXT, NY), f32),
            vmem((CX, 5, KV, NY), f32),
            vmem((CX, 2 * KV, 3 * NY), bf16),
            vmem((CX, 2 * KV, 2 * NY), bf16),
            vmem((EXT // GROUP, 2 * KV, GROUP * NY), bf16),
            vmem((EXT // GROUP, 2 * KV, GROUP * NY), bf16),
            vmem((n_sub // 2, 2, MSG, NY), f32),
            pltpu.SemaphoreType.DMA((2,)),
            pltpu.SemaphoreType.DMA((16,)),
            pltpu.SemaphoreType.DMA((16,)),
            pltpu.SemaphoreType.DMA,
            pltpu.SemaphoreType.DMA((n_sub // 2,)),
            pltpu.SemaphoreType.DMA,
            pltpu.SemaphoreType.DMA,
            pltpu.SemaphoreType.REGULAR,
        ],
        compiler_params=pltpu.CompilerParams(
            collective_id=0, has_side_effects=True, vmem_limit_bytes=58 << 20
        ),
    )(jnp.transpose(vectors, (0, 2, 1, 3)), permeability, counts, ownership)


def solution(mesh):
    in_specs = (P(None, "grp", "sub", None), P("grp", "sub", None), P("grp", "sub"), P("grp", None))
    out_specs = P("grp", None, None, None)
    return jax.shard_map(
        functools.partial(per_device, mesh.shape["grp"], mesh.shape["sub"]),
        mesh=mesh, in_specs=in_specs, out_specs=out_specs, check_vma=False,
    )
```

```python
import functools

import jax
import jax.numpy as jnp
from jax import lax
from jax.experimental import pallas as pl
from jax.experimental.pallas import tpu as pltpu
from jax.sharding import PartitionSpec as P

MESH = pl.DeviceIdType.MESH
KV = 16
OV = 2
CX = 16
CZ = 16
NY = 128
EXT = CZ + 2 * OV
GROUP = 4
MSG = 24


def harmonic(first_perm, second_perm):
    return 2.0 * first_perm * second_perm / (first_perm + second_perm)


def split(values):
    high = values.astype(jnp.bfloat16)
    low = (values - high.astype(jnp.float32)).astype(jnp.bfloat16)
    return high, low


def stack_split(values):
    pairs = [split(value) for value in values]
    high = jnp.concatenate([pair[0] for pair in pairs], axis=1)
    low = jnp.concatenate([pair[1] for pair in pairs], axis=1)
    return jnp.concatenate([high, low], axis=0)


def gram(first, second):
    return lax.dot_general(
        first, second, (((1,), (1,)), ((), ())), preferred_element_type=jnp.float32
    )


def fold(product):
    return (product[:KV, :KV] + product[:KV, KV:]) + (product[KV:, :KV] + product[KV:, KV:])


def assemble_kernel(n_grp, n_sub, vec, perm, counts, ownership, out, z, zup, zdn, xl, xr, xd,
                    pown, pzl, pzu, pxl, pxr, pc, fx, fz, fy, dg, ends, ex, ez, ey, ed, rim,
                    raw, wp1, wp2, wl, wr, pool,
                    load_sem, send_sem, recv_sem, all_send, all_recv, pair_send, pair_recv, known):
    s = lax.axis_index("sub")
    g = lax.axis_index("grp")
    up, down = lax.rem(s + 1, n_sub), lax.rem(s + n_sub - 1, n_sub)
    chip, core = s // 2, lax.rem(s, 2)
    n_chip = n_sub // 2
    mate = chip * 2 + 1 - core
    right, left = lax.rem(g + 1, n_grp), lax.rem(g + n_grp - 1, n_grp)

    for a in range(KV):
        pltpu.make_async_copy(
            vec.at[a], z.at[:, pl.ds(1, CX), a, :], load_sem.at[0]
        ).start()
    pltpu.make_async_copy(perm, pown, load_sem.at[1]).start()

    barrier = pltpu.get_barrier_semaphore()
    has_left, has_right = g > 0, g < n_grp - 1
    for there, tg in ((has_left, left), (has_right, right)):
        @pl.when(there)
        def _(tg=tg):
            for ts in (s, up, down):
                pl.semaphore_signal(barrier, inc=1, device_id=(tg, ts), device_id_type=MESH)
    for reach in (1, 2, 4):
        for ts in (lax.rem(s + reach, n_sub), lax.rem(s + n_sub - reach, n_sub)):
            pl.semaphore_signal(barrier, inc=1, device_id=(g, ts), device_id_type=MESH)

    zero_block = jnp.zeros((KV, NY), jnp.float32)
    for missing, face, ring, near in (
        (g == 0, pxl, xl, (0, 1)), (g == n_grp - 1, pxr, xr, (2, 3))
    ):
        @pl.when(missing)
        def _(face=face, ring=ring, near=near):
            face[...] = jnp.zeros(face.shape, jnp.float32)
            ring[...] = jnp.zeros(ring.shape, jnp.float32)
            for i in near:
                pc[i] = jnp.zeros(pc.shape[1:], jnp.float32)
                xd[i] = jnp.zeros(xd.shape[1:], jnp.float32)

    for r in range(EXT):
        z[r, 0] = zero_block
        z[r, CX + 1] = zero_block

    at_low, at_high = s == 0, s == n_sub - 1
    at_left, at_right = g == 0, g == n_grp - 1
    lane = lax.broadcasted_iota(jnp.int32, (CZ, NY), 1)
    level = lax.broadcasted_iota(jnp.int32, (CZ, NY), 0)

    def along_y(cells, lanes):
        upward = harmonic(cells, pltpu.roll(cells, NY - 1, 1))
        coupling = jnp.where(lanes == NY - 1, 0.0, upward)
        both = jnp.where(lanes == NY - 1, cells, upward) + jnp.where(
            lanes == 0, cells, pltpu.roll(upward, 1, 1)
        )
        return coupling, both

    pltpu.make_async_copy(perm, pown, load_sem.at[1]).wait()
    fx[0] = jnp.zeros((CZ, NY), jnp.float32)
    fx[CX] = jnp.zeros((CZ, NY), jnp.float32)

    def inner_faces(x, carry):
        fx[x] = harmonic(pown[x - 1], pown[x])
        return carry

    lax.fori_loop(1, CX, inner_faces, 0, unroll=5)

    def inner_coefficients(x, carry):
        own = pown[x]
        upward = jnp.where(level == CZ - 1, 0.0, harmonic(own, pltpu.roll(own, CZ - 1, 0)))
        coupling, both = along_y(own, lane)
        fz[x] = upward
        fy[x] = coupling
        dg[x] = (fx[x] + fx[x + 1]) + (upward + pltpu.roll(upward, 1, 0)) + both
        return carry

    lax.fori_loop(0, CX, inner_coefficients, 0, unroll=8)

    pl.semaphore_wait(
        barrier, 6 + 3 * has_left.astype(jnp.int32) + 3 * has_right.astype(jnp.int32)
    )

    def send(slot, src, dst, tg, ts):
        copy = pltpu.make_async_remote_copy(
            src_ref=src, dst_ref=dst, send_sem=send_sem.at[slot], recv_sem=recv_sem.at[slot],
            device_id=(tg, ts), device_id_type=MESH,
        )
        return copy

    half = CZ // 2
    perm_copies = [
        send(0, perm.at[:, pl.ds(CZ - 3, 3), :], pzl, g, up),
        send(1, perm.at[:, pl.ds(0, 3), :], pzu, g, down),
        send(2, perm.at[CX - 1], pxl, right, s),
        send(3, perm.at[0], pxr, left, s),
        send(4, perm.at[CX - 1, pl.ds(half, half), :], pc.at[0], right, up),
        send(5, perm.at[CX - 1, pl.ds(0, half), :], pc.at[1], right, down),
        send(6, perm.at[0, pl.ds(half, half), :], pc.at[2], left, up),
        send(7, perm.at[0, pl.ds(0, half), :], pc.at[3], left, down),
    ]
    vec_copies = [
        send(8, z.at[pl.ds(0, 3), pl.ds(1, CX)], zup, g, down),
        send(9, z.at[pl.ds(EXT - 2, 2), pl.ds(1, CX)], zdn, g, up),
        send(10, z.at[:, 1], xr, left, s),
        send(11, z.at[:, CX], xl, right, s),
        send(12, z.at[pl.ds(EXT - 4, 4), CX], xd.at[0], right, up),
        send(13, z.at[pl.ds(0, 4), CX], xd.at[1], right, down),
        send(14, z.at[pl.ds(EXT - 4, 4), 1], xd.at[2], left, up),
        send(15, z.at[pl.ds(0, 4), 1], xd.at[3], left, down),
    ]
    copies = perm_copies + vec_copies
    to_left, to_right = (3, 6, 7, 10, 14, 15), (2, 4, 5, 11, 12, 13)
    along = [i for i in range(len(copies)) if i not in to_left + to_right]
    def start_all(group):
        for slots, there in ((along, None), (to_left, has_left), (to_right, has_right)):
            def start(slots=slots):
                for i in slots:
                    if i in group:
                        copies[i].start()

            start() if there is None else pl.when(there)(start)

    def received(group):
        for slots, there in ((along, None), (to_right, has_left), (to_left, has_right)):
            def wait(slots=slots):
                for i in slots:
                    if i in group:
                        copies[i].wait_recv()

            wait() if there is None else pl.when(there)(wait)

    def sent():
        for slots, there in ((along, None), (to_left, has_left), (to_right, has_right)):
            def wait(slots=slots):
                for i in slots:
                    copies[i].wait_send()

            wait() if there is None else pl.when(there)(wait)

    start_all(range(8))
    whole = z.at[:, pl.ds(1, CX)]
    pltpu.make_async_copy(whole, whole, load_sem.at[0]).wait()
    count = counts[0, 0]
    own_rows = (lax.broadcasted_iota(jnp.int32, (KV, NY), 0) < count).astype(jnp.float32)
    low_keep = own_rows * (s > 0).astype(jnp.float32)
    high_keep = own_rows * (s < n_sub - 1).astype(jnp.float32)

    def keep_of(r):
        return low_keep if r < OV else high_keep if r >= EXT - OV else own_rows

    def mask_ends(x, carry):
        for r in (0, 1, 2, EXT - 2, EXT - 1):
            z[r, x] = z[r, x] * keep_of(r)
        return carry

    lax.fori_loop(1, CX + 1, mask_ends, 0, unroll=4)

    start_all((8, 9))

    def mask_sides(r, carry):
        z[r, 1] = z[r, 1] * own_rows
        z[r, CX] = z[r, CX] * own_rows
        return carry

    lax.fori_loop(3, EXT - 2, mask_sides, 0, unroll=5)

    start_all(range(10, 16))
    for ts in (lax.rem(s + 4, n_sub), lax.rem(s + n_sub - 4, n_sub)):
        pl.semaphore_signal(known, inc=1, device_id=(g, ts), device_id_type=MESH)

    def column(x, total):
        for first in range(0, CZ, GROUP):
            mine, applied = [], []
            for i in range(first, first + GROUP):
                r = i + OV
                here = z[r, x + 1]
                along = fy[x, i : i + 1, :]
                result = dg[x, i : i + 1, :] * here
                result = result - fx[x, i : i + 1, :] * z[r, x]
                result = result - fx[x + 1, i : i + 1, :] * z[r, x + 2]
                if i > 0:
                    result = result - fz[x, i - 1 : i, :] * z[r - 1, x + 1]
                if i < CZ - 1:
                    result = result - fz[x, i : i + 1, :] * z[r + 1, x + 1]
                result = result - along * pltpu.roll(here, NY - 1, 1)
                result = result - pltpu.roll(along * here, 1, 1)
                mine.append(here)
                applied.append(result)
                if i < 2:
                    raw[x, i] = result
                if i >= CZ - 2:
                    raw[x, i - CZ + 4] = result
            total = total + gram(stack_split(mine), stack_split(applied))
        return total

    total = jnp.zeros((2 * KV, 2 * KV), jnp.float32)
    total = lax.fori_loop(0, 4, column, total, unroll=2)
    total = lax.fori_loop(4, CX, column, total, unroll=2)

    received(range(8))

    def gather_ends(x, carry):
        own = pown[x]
        first, last = own[0:1], own[CZ - 1 : CZ]
        low = jnp.where(at_low, jnp.broadcast_to(first, (3, NY)), pzl[x])
        high = jnp.where(at_high, jnp.broadcast_to(last, (3, NY)), pzu[x])
        ends[x, 0:3] = low
        ends[x, 3:4] = first
        ends[x, 4:5] = last
        ends[x, 5:8] = high
        return carry

    lax.fori_loop(0, CX, gather_ends, 0, unroll=8)
    ex[0] = jnp.zeros((8, NY), jnp.float32)
    ex[CX] = jnp.zeros((8, NY), jnp.float32)

    def end_faces(x, carry):
        ex[x] = harmonic(ends[x - 1], ends[x])
        return carry

    lax.fori_loop(1, CX, end_faces, 0, unroll=15)

    def end_coefficients(x, carry):
        own = ends[x]
        upward = harmonic(own, pltpu.roll(own, 7, 0))
        coupling, both = along_y(own, lane[0:8])
        ez[x] = upward
        ey[x] = coupling
        ed[x] = (ex[x] + ex[x + 1]) + (upward + pltpu.roll(upward, 1, 0)) + both
        return carry

    lax.fori_loop(0, CX, end_coefficients, 0, unroll=16)
    for side, at_edge, own_x, face, low, high in (
        (0, at_left, 0, pxl, 0, 1), (1, at_right, CX - 1, pxr, 2, 3)
    ):
        rim[side, 2 : 2 + CZ] = harmonic(
            pown[own_x], jnp.where(at_edge, pown[own_x], face[...])
        )
        own = ends[own_x, 1:3]
        rim[side, 0:2] = harmonic(own, jnp.where(at_edge, own, pc[low, half - 2 : half]))
        own = ends[own_x, 5:7]
        rim[side, EXT - 2 : EXT] = harmonic(own, jnp.where(at_edge, own, pc[high, 0:2]))

    not_high = 1.0 - at_high.astype(jnp.float32)

    def end_column(x, total):
        mine = {r: z[r, x + 1] for r in (0, 1, 2, EXT - 3, EXT - 2, EXT - 1)}
        applied = {}
        for r, i in ((0, 1), (1, 2), (EXT - 2, 5), (EXT - 1, 6)):
            here = mine[r]
            along = ey[x, i : i + 1, :]
            result = ed[x, i : i + 1, :] * here
            result = result - ex[x, i : i + 1, :] * z[r, x]
            result = result - ex[x + 1, i : i + 1, :] * z[r, x + 2]
            if r > 0:
                result = result - ez[x, i - 1 : i, :] * mine[r - 1]
            if r < EXT - 1:
                result = result - ez[x, i : i + 1, :] * mine[r + 1]
            result = result - along * pltpu.roll(here, NY - 1, 1)
            applied[r] = result - pltpu.roll(along * here, 1, 1)
        low_face, high_face = ez[x, 2:3, :], ez[x, 4:5, :]
        applied[2] = low_face * (mine[2] - mine[1])
        kept = high_face * mine[EXT - 3]
        applied[EXT - 3] = kept - high_face * mine[EXT - 2]
        raw[x, 0] = raw[x, 0] + applied[2]
        raw[x, 3] = raw[x, 3] + kept
        raw[x, 4] = -(kept * not_high)
        order = sorted(mine)
        return total + gram(
            stack_split([mine[r] for r in order]), stack_split([applied[r] for r in order])
        )

    total = lax.fori_loop(0, CX, end_column, total, unroll=4)

    for target, side, row in ((wl, 0, 1), (wr, 1, CX)):
        def side_weight(i, total, target=target, side=side, row=row):
            mine, weight = [], []
            for k in range(GROUP):
                here = z[i * GROUP + k, row]
                mine.append(here)
                weight.append(rim[side, pl.ds(i * GROUP + k, 1), :] * here)
            weight = stack_split(weight)
            target[i] = weight
            return total + gram(stack_split(mine), weight)

        total = lax.fori_loop(0, EXT // GROUP, side_weight, total, unroll=5)
        for i, r in ((0, 2), (1, 3), (2, EXT - 4), (3, EXT - 3)):
            raw[row - 1, i] = raw[row - 1, i] + rim[side, r : r + 1, :] * z[r, row]

    def finish_weights(x, carry):
        wp2[x] = stack_split([raw[x, 0], raw[x, 1]])
        wp1[x] = stack_split([raw[x, 2], raw[x, 3], raw[x, 4]])
        return carry

    lax.fori_loop(0, CX, finish_weights, 0, unroll=8)

    row_keep = lax.broadcasted_iota(jnp.int32, (KV, KV), 0) < count
    col_keep = lax.broadcasted_iota(jnp.int32, (KV, KV), 1) < count
    blocks = {4: jnp.where(row_keep & col_keep, fold(total), 0.0)}

    received((8,))

    def upper_pair(x, carry):
        theirs = stack_split([zup[0, x], zup[1, x], zup[2, x]])
        return carry[0] + gram(wp1[x], theirs), carry[1] + gram(theirs, wp1[x])

    zeros = jnp.zeros((2 * KV, 2 * KV), jnp.float32)
    straight, turned = lax.fori_loop(0, CX, upper_pair, (zeros, zeros), unroll=16)
    blocks[5] = jnp.where(row_keep, fold(straight), 0.0)
    blocks[9] = jnp.where(col_keep, fold(turned), 0.0)

    received((9,))

    def lower_pair(x, carry):
        theirs = stack_split([zdn[0, x], zdn[1, x]])
        return carry[0] + gram(wp2[x], theirs), carry[1] + gram(theirs, wp2[x])

    straight, turned = lax.fori_loop(0, CX, lower_pair, (zeros, zeros), unroll=16)
    blocks[3] = jnp.where(row_keep, fold(straight), 0.0)
    blocks[10] = jnp.where(col_keep, fold(turned), 0.0)

    received(range(10, 16))
    left_on = -(1.0 - at_left.astype(jnp.float32))
    right_on = -(1.0 - at_right.astype(jnp.float32))
    for base, on, weight, face, low, high in ((0, left_on, wl, xl, 0, 1), (6, right_on, wr, xr, 2, 3)):
        def side_pair(i, total, weight=weight, face=face):
            theirs = stack_split([face[i * GROUP + k] for k in range(GROUP)])
            return total + gram(weight[i], theirs)

        product = lax.fori_loop(0, EXT // GROUP, side_pair, zeros, unroll=5)
        blocks[base + 1] = jnp.where(row_keep, fold(product) * on, 0.0)
        theirs = stack_split([xd[low, r] for r in range(4)])
        blocks[base] = jnp.where(row_keep, fold(gram(weight[0], theirs)) * on, 0.0)
        theirs = stack_split([xd[high, r] for r in range(4)])
        blocks[base + 2] = jnp.where(
            row_keep, fold(gram(weight[EXT // GROUP - 1], theirs)) * on, 0.0
        )

    msg = pool.at[chip, core]
    msg[0:KV, :] = jnp.concatenate([blocks[i] for i in range(8)], axis=1)
    half_v = KV // 2
    gap = jnp.zeros((half_v, KV), jnp.float32)
    parts = [blocks[8][:half_v], blocks[8][half_v:], gap, blocks[9][:half_v], blocks[9][half_v:],
             blocks[10][:half_v], blocks[10][half_v:], gap]
    msg[KV:, :] = jnp.concatenate(parts, axis=1)

    pl.semaphore_wait(known, 2)

    def pass_on(origin, hops):
        slot = pool.at[lax.rem(chip + n_chip + origin, n_chip), core]
        pltpu.make_async_remote_copy(
            src_ref=slot, dst_ref=slot, send_sem=all_send,
            recv_sem=all_recv.at[(origin - hops) % n_chip],
            device_id=(g, lax.rem(s + n_sub + 2 * hops, n_sub)), device_id_type=MESH,
        ).start()

    def arrived(origin):
        slot = pool.at[lax.rem(chip + n_chip + origin, n_chip), core]
        pltpu.make_async_copy(slot, slot, all_recv.at[origin % n_chip]).wait()

    def hand_over(origin):
        slot = pool.at[lax.rem(chip + n_chip + origin, n_chip), core]
        pltpu.make_async_remote_copy(
            src_ref=slot, dst_ref=slot, send_sem=pair_send, recv_sem=pair_recv,
            device_id=(g, mate), device_id_type=MESH,
        ).start()

    for hops in (4, -4, 2, -2, 1, -1):
        pass_on(0, hops)
    hand_over(0)
    arrived(-4)

    @pl.when(core == 0)
    def _():
        pass_on(-4, 4)

    for hops in (3, 2, 1, -1):
        pass_on(-4, hops)

    arrived(4)

    @pl.when(core == 1)
    def _():
        pass_on(4, -4)

    for hops in (-3, -2, -1, 1):
        pass_on(4, hops)

    hand_over(-4)
    hand_over(4)
    for origin in (1, -1, 2, -2, 3, -3, 5, -5, 6, -6, 7, -7, 8):
        arrived(origin)
        hand_over(origin)
    sent()
    theirs = pool.at[:, 0]
    pltpu.make_async_copy(theirs, theirs, pair_recv).wait()

    lane = lax.broadcasted_iota(jnp.int32, (half_v, NY), 1)
    from_below = (lane >= 3 * KV) & (lane < 4 * KV)
    from_above = (lane >= 5 * KV) & (lane < 6 * KV)

    def place(j, carry):
        row = ownership[0, j]
        before, after = jnp.maximum(row - 1, 0), jnp.minimum(row + 1, n_sub - 1)
        below = pool[before // 2, lax.rem(before, 2), KV:, :]
        above = pool[after // 2, lax.rem(after, 2), KV:, :]
        extra = pool[row // 2, lax.rem(row, 2), KV:, :]
        added = jnp.where(from_below & (row > 0), below, 0.0)
        added = added + jnp.where(from_above & (row < n_sub - 1), above, 0.0)
        top = pool[row // 2, lax.rem(row, 2), :half_v, :]
        bottom = pool[row // 2, lax.rem(row, 2), half_v:KV, :]
        shift = NY - KV
        below = pltpu.roll(below, shift, 1)
        above = pltpu.roll(above, shift, 1)
        out[0, j, :half_v, NY:] = extra[:, :KV]
        out[0, j, half_v:, NY:] = pltpu.roll(extra, shift, 1)[:, :KV]
        out[0, j, :half_v, 0:NY] = top + added
        added = jnp.where(from_below & (row > 0), below, 0.0)
        added = added + jnp.where(from_above & (row < n_sub - 1), above, 0.0)
        out[0, j, half_v:, 0:NY] = bottom + added
        return carry

    lax.fori_loop(0, n_sub, place, 0, unroll=8)
    rest = pool.at[pl.ds(0, n_chip - 1), 0]
    pltpu.make_async_copy(theirs, theirs, pair_send).wait()
    pltpu.make_async_copy(rest, rest, all_send).wait()


def per_device(n_grp, n_sub, vectors, permeability, counts, ownership):
    f32, bf16 = jnp.float32, jnp.bfloat16
    vmem = pltpu.VMEM
    return pl.pallas_call(
        functools.partial(assemble_kernel, n_grp, n_sub),
        out_shape=jax.ShapeDtypeStruct((1, n_sub, KV, 9 * KV), f32),
        in_specs=[
            pl.BlockSpec(memory_space=pl.ANY),
            pl.BlockSpec(memory_space=pl.ANY),
            pl.BlockSpec(memory_space=pltpu.SMEM),
            pl.BlockSpec(memory_space=pltpu.SMEM),
        ],
        out_specs=pl.BlockSpec(memory_space=pltpu.VMEM),
        scratch_shapes=[
            vmem((EXT, CX + 2, KV, NY), f32),
            vmem((3, CX, KV, NY), f32),
            vmem((2, CX, KV, NY), f32),
            vmem((EXT, KV, NY), f32),
            vmem((EXT, KV, NY), f32),
            vmem((4, 4, KV, NY), f32),
            vmem((CX, CZ, NY), f32),
            vmem((CX, 3, NY), f32),
            vmem((CX, 3, NY), f32),
            vmem((CZ, NY), f32),
            vmem((CZ, NY), f32),
            vmem((4, CZ // 2, NY), f32),
            vmem((CX + 1, CZ, NY), f32),
            vmem((CX, CZ, NY), f32),
            vmem((CX, CZ, NY), f32),
            vmem((CX, CZ, NY), f32),
            vmem((CX, 8, NY), f32),
            vmem((CX + 1, 8, NY), f32),
            vmem((CX, 8, NY), f32),
            vmem((CX, 8, NY), f32),
            vmem((CX, 8, NY), f32),
            vmem((2, EXT, NY), f32),
            vmem((CX, 5, KV, NY), f32),
            vmem((CX, 2 * KV, 3 * NY), bf16),
            vmem((CX, 2 * KV, 2 * NY), bf16),
            vmem((EXT // GROUP, 2 * KV, GROUP * NY), bf16),
            vmem((EXT // GROUP, 2 * KV, GROUP * NY), bf16),
            vmem((n_sub // 2, 2, MSG, NY), f32),
            pltpu.SemaphoreType.DMA((2,)),
            pltpu.SemaphoreType.DMA((16,)),
            pltpu.SemaphoreType.DMA((16,)),
            pltpu.SemaphoreType.DMA,
            pltpu.SemaphoreType.DMA((n_sub // 2,)),
            pltpu.SemaphoreType.DMA,
            pltpu.SemaphoreType.DMA,
            pltpu.SemaphoreType.REGULAR,
        ],
        compiler_params=pltpu.CompilerParams(
            collective_id=0, has_side_effects=True, vmem_limit_bytes=58 << 20
        ),
    )(jnp.transpose(vectors, (0, 2, 1, 3)), permeability, counts, ownership)


def solution(mesh):
    in_specs = (P(None, "grp", "sub", None), P("grp", "sub", None), P("grp", "sub"), P("grp", None))
    out_specs = P("grp", None, None, None)
    return jax.shard_map(
        functools.partial(per_device, mesh.shape["grp"], mesh.shape["sub"]),
        mesh=mesh, in_specs=in_specs, out_specs=out_specs, check_vma=False,
    )
```
